32 devices in a mesh: grp: 8 (over y, x, core), ep: 4 (over z).
Axes of the slice: x: 2, y: 2, z: 4, core: 2. Of those that a mesh axis runs over, the one named last changes fastest.
Arguments:
- queries: bfloat16 [128, 2304], P('grp'), may hold values from -36 to 36, as said below
- residual: bfloat16 [128, 2304], P(('grp', 'ep')), may hold values from -20 to 20
- gain: bfloat16 [2304], replicated, may hold values from 0.5 to 1.5
- key_pages: bfloat16 [256, 128, 2304], P(('grp', 'ep')), may hold values from -6 to 6
- value_pages: bfloat16 [256, 128, 2304], P(('grp', 'ep')), may hold values from -6 to 6
- page_table: int32 [128, 16], P('grp'), may hold values from -1 to 31, as said below
- lengths: int32 [128], P('grp'), may hold values from 1 to 2048, as said below
- split_flag: int32 [128], P('grp'), may hold values from 0 to 1, as said below
- routes: int32 [128, 2], P(('grp', 'ep')), may hold values from 0 to 3, all different within a row; in each aligned block of 4 rows (0 to 3, 4 to 7, ...) at most 2 rows name the same one
- gates: bfloat16 [128, 2], P(('grp', 'ep')), may hold values from 0.19921875 to 1
- w_gate: bfloat16 [4, 2304, 5760], P('ep', None, 'grp'), may hold values from -0.125 to 0.125
- w_up: bfloat16 [4, 2304, 5760], P('ep', None, 'grp'), may hold values from -0.125 to 0.125
- w_down: bfloat16 [4, 5760, 2304], P('ep', 'grp'), may hold values from -0.078125 to 0.078125
Outputs:
- update: bfloat16 [128, 2304], P(('grp', 'ep'))
The draws below stay inside these ranges and needn't reach their ends.
Inputs may be any that keep to these rules, and one draw needn't show every extreme that they name: `page_table`: entries j with j * 128 < lengths[r] are pages of the row's group; no page is named twice within a group; the other entries are -1. `lengths`: A split request's first half, in the even group of its pair, is always 16 * 128 tokens; other rows are no longer. `split_flag`: in every group exactly one row is 1, at the same slot in both groups of each pair 2i, 2i + 1. `routes`: within the rows of one device no expert is named more than 2 times. `queries`: the two rows of a split request hold the same query.
All inputs are finite; a program needn't handle non-finite values.
Results may differ from the reference program's by a relative error of at most 0.015.
Values may be sent and summed in bfloat16 or wider, within the bound.
A program may use at most 192 MiB of HBM per device.

```python
import math
import jax
import jax.numpy as jnp
import numpy as np
from jax import lax

HEADS = 36
HEAD_DIM = 64
D = 2304
FF = 5760
EXPERTS = 4
PAGE = 128
REQ_DEV = 4
PAGES_DEV = 8
LONG_PAGES = 16
CAP = 2
ROWS = 128
PAGES_ALL = 256
N_GRP = 8
N_EP = 4


def layout_draw(key):
    pair_count = N_GRP // 2
    pool_size = PAGES_DEV * N_EP
    group_rows = REQ_DEV * N_EP
    split_slot = jax.random.randint(jax.random.fold_in(key, 11), (pair_count,), 0, group_rows).astype(jnp.int32)
    tail_length = jax.random.randint(jax.random.fold_in(key, 12), (pair_count,), 1, LONG_PAGES * PAGE + 1).astype(jnp.int32)
    short_length = jax.random.randint(jax.random.fold_in(key, 13), (N_GRP, group_rows), 1, PAGE + 1).astype(jnp.int32)
    group_keys = jax.random.split(jax.random.fold_in(key, 14), N_GRP)
    orders = jax.vmap(lambda group_key: jax.random.permutation(group_key, pool_size))(group_keys).astype(jnp.int32)
    first_entry = orders[:, :1]
    orders = jnp.where(orders == pool_size - 1, first_entry, orders)
    column_ids = jnp.arange(pool_size, dtype=jnp.int32)
    orders = jnp.where(column_ids[None, :] == 0, pool_size - 1, orders).astype(jnp.int32)
    group_ids = jnp.arange(N_GRP, dtype=jnp.int32)
    slot_ids = jnp.arange(group_rows, dtype=jnp.int32)
    chosen = split_slot[group_ids // 2]
    is_split = slot_ids[None, :] == chosen[:, None]
    is_odd = (group_ids % 2 == 1)[:, None]
    long_length = jnp.where(is_odd, tail_length[group_ids // 2][:, None], LONG_PAGES * PAGE)
    row_lengths = jnp.where(is_split, long_length, short_length).astype(jnp.int32)
    ranking = slot_ids[None, :] - (slot_ids[None, :] > chosen[:, None]).astype(jnp.int32)
    short_page = jnp.take_along_axis(orders, LONG_PAGES + ranking, axis=1)
    table_steps = jnp.arange(LONG_PAGES, dtype=jnp.int32)
    long_pages = orders[:, :LONG_PAGES]
    short_rows = jnp.where(table_steps[None, None, :] == 0, short_page[:, :, None], -1)
    page_rows = jnp.where(is_split[:, :, None], long_pages[:, None, :], short_rows)
    live_step = table_steps[None, None, :] * PAGE < row_lengths[:, :, None]
    page_rows = jnp.where(live_step, page_rows, -1).astype(jnp.int32)
    return (page_rows.reshape(ROWS, LONG_PAGES), row_lengths.reshape(ROWS), is_split.astype(jnp.int32).reshape(ROWS))


def draw_page_table(key, part):
    return layout_draw(key)[0]


def draw_lengths(key, part):
    return layout_draw(key)[1]


def draw_split_flag(key, part):
    return layout_draw(key)[2]


def draw_queries(key, part):
    base = jax.random.normal(jax.random.fold_in(key, 1), (ROWS, D), jnp.float32)
    base = jnp.clip(base, -36.0, 36.0)
    split_rows = layout_draw(key)[2]
    grouped = base.reshape(N_GRP // 2, 2, REQ_DEV * N_EP, D)
    flags = split_rows.reshape(N_GRP // 2, 2, REQ_DEV * N_EP)[:, 1]
    second = jnp.where(flags[..., None] == 1, grouped[:, 0], grouped[:, 1])
    joined = jnp.stack([grouped[:, 0], second], axis=1)
    return joined.reshape(ROWS, D).astype(jnp.bfloat16)


def draw_key_pages(key, part):
    base = jax.random.normal(jax.random.fold_in(key, 2), (PAGES_ALL, PAGE, D), jnp.float32)
    return jnp.clip(base, -6.0, 6.0).astype(jnp.bfloat16)


def draw_residual(key, part):
    row_scale = jnp.exp(jax.random.uniform(jax.random.fold_in(key, 21), (ROWS, 1), jnp.float32, jnp.log(0.3), jnp.log(3.0)))
    col_scale = jnp.exp(jax.random.uniform(jax.random.fold_in(key, 22), (1, D), jnp.float32, jnp.log(0.5), jnp.log(2.0)))
    base = jax.random.normal(jax.random.fold_in(key, 23), (ROWS, D), jnp.float32)
    return jnp.clip(base * row_scale * col_scale, -20.0, 20.0).astype(jnp.bfloat16)


def block_scale(own_key, extent, pieces, smallest, top_value):
    def one(axis_at, blocks):
        draws = jax.random.uniform(jax.random.fold_in(jax.random.fold_in(own_key, 6), axis_at), (blocks,), jnp.float32, smallest / len(pieces), top_value / len(pieces))
        return jnp.repeat(jnp.exp(draws), extent[axis_at] // blocks).reshape((-1,) + (1,) * (len(extent) - axis_at - 1))

    factor_of = one(*pieces[0])
    for cut in pieces[1:]:
        factor_of = factor_of * one(*cut)
    return factor_of


def shared_out(stream_key, own, number, rows, number_of, top, bound, slope):
    order = jax.random.permutation(stream_key, number_of)
    heavy_load, usual = load_shares(number_of, rows * top, bound, slope, True), load_shares(number_of, rows * top, bound, slope, False)
    places = jnp.arange(number_of)

    def named(sizes, turn):
        used = int((sizes > 0).sum())
        fixed = max(1, used // 4)
        passed = fixed + (places - fixed + turn * (used - fixed)) % max(1, number_of - fixed)
        return jnp.zeros((number_of,), jnp.int32).at[order[jnp.where(places < fixed, places, passed)]].set(jnp.asarray(sizes, jnp.int32))

    sizes = jnp.where(number % 4 == 0, named(heavy_load, number // 4), named(usual, number - number // 4 - 1))
    mixed = jax.random.permutation(jax.random.fold_in(own, 3), number_of)
    donor, receiver = mixed[0:number_of // 2 * 2:2], mixed[1:number_of // 2 * 2:2]
    slack = jnp.minimum(sizes[donor] - 1, bound - sizes[receiver]) // 2
    slack = jnp.where((donor == order[0]) | (receiver == order[0]) | (sizes[receiver] == 0), 0, jnp.maximum(slack, 0))
    passed = jax.random.randint(jax.random.fold_in(own, 4), (number_of // 2,), 0, 1 << 20) % (slack + 1)
    sizes = sizes.at[donor].add(-passed).at[receiver].add(passed)
    members = jnp.searchsorted(jnp.cumsum(sizes), jnp.arange(rows * top), side="right").astype(jnp.int32)
    listing = members.reshape(top, rows).T
    listing = listing[jax.random.permutation(jax.random.fold_in(own, 1), rows)]
    turn = jax.random.randint(jax.random.fold_in(own, 2), (rows, 1), 0, top)
    return jnp.take_along_axis(listing, (jnp.arange(top)[None, :] + turn) % top, axis=1)


def load_shares(amount, total, limit, skew, full):
    weights = [(1 << 20) // math.isqrt(rank ** skew) + 1 for rank in range(1, amount + 1)]
    largest = limit if full else min(limit, max(-(-total // amount), total * weights[0] // sum(weights)))
    least = 1 if total - largest >= amount - 1 else 0
    given, rest = [largest] + [least] * (amount - 1), total - largest - least * (amount - 1)
    while rest > 0:
        candidates = [i for i in range(1, amount) if given[i] < largest] or [i for i in range(1, amount) if given[i] < limit]
        pool, remaining = sum([weights[i] for i in candidates]), rest
        for i in candidates:
            extra = min(limit - given[i], max(1, remaining * weights[i] // pool), rest)
            given[i] = given[i] + extra
            rest = rest - extra
    return np.array(given)


def centred(rng, shape, scale, limit, cuts=(), kind=jnp.bfloat16):
    result = scale * jax.random.normal(rng, shape, jnp.float32)
    if cuts:
        result = result * block_scale(rng, shape, cuts, -0.22, 0.18)
    return jnp.clip(result, -limit, limit).astype(kind)


def setup_inputs(seed: int = 0) -> dict:
    splits = jax.random.split(jax.random.key(seed), 14)
    queries = draw_queries(jax.random.fold_in(splits[13], 71), 0)
    residual = draw_residual(jax.random.fold_in(splits[13], 71), 0)
    gain = jnp.clip(1.0 + 0.1 * jax.random.normal(splits[2], (D,), jnp.float32), 0.5, 1.5).astype(jnp.bfloat16)
    key_pages = draw_key_pages(jax.random.fold_in(splits[13], 71), 0)
    value_pages = centred(splits[4], (PAGES_ALL, PAGE, D), 1.0, 6.0, ((0, 32),))
    page_table = draw_page_table(jax.random.fold_in(splits[13], 71), 0)
    lengths = draw_lengths(jax.random.fold_in(splits[13], 71), 0)
    split_flag = draw_split_flag(jax.random.fold_in(splits[13], 71), 0)
    routes_keys = jax.random.split(jax.random.fold_in(splits[8], 1), ROWS // REQ_DEV)
    routes_turns = jax.random.permutation(jax.random.fold_in(splits[8], 3), ROWS // REQ_DEV)
    routes = jax.vmap(lambda own, number: shared_out(jax.random.fold_in(splits[8], 2), own, number, REQ_DEV, EXPERTS, 2, CAP, 2))(routes_keys, routes_turns).reshape((ROWS, 2))
    gates = jnp.clip(0.19921875 + 0.80078125 * jax.random.uniform(splits[9], (ROWS, 2), jnp.float32) ** block_scale(splits[9], (ROWS, 2), ((0, 32),), -0.2, 0.2), 0.19921875, 1.0).astype(jnp.bfloat16)
    w_gate = centred(splits[10], (EXPERTS, D, FF), D ** -0.5, 0.125, ((0, 4), (2, 8)))
    w_up = centred(splits[11], (EXPERTS, D, FF), D ** -0.5, 0.125, ((0, 4), (2, 8)))
    w_down = centred(splits[12], (EXPERTS, FF, D), FF ** -0.5, 0.078125, ((0, 4), (1, 8)))
    return {"queries": queries, "residual": residual, "gain": gain, "key_pages": key_pages, "value_pages": value_pages, "page_table": page_table, "lengths": lengths, "split_flag": split_flag, "routes": routes, "gates": gates, "w_gate": w_gate, "w_up": w_up, "w_down": w_down}


NEG_FILL = -1e+30
NORM_EPS = 1e-06

def merge_parts(first_part, second_part):
    maxima_a, totals_a, weighted_a = first_part
    maxima_b, totals_b, weighted_b = second_part
    highest = jnp.maximum(maxima_a, maxima_b)
    factor_a = jnp.exp(maxima_a - highest)
    factor_b = jnp.exp(maxima_b - highest)
    head_count = maxima_a.shape[-1]
    shaped = weighted_a.shape
    wide = shaped[:-1] + (head_count, shaped[-1] // head_count)
    weighted = weighted_a.reshape(wide) * factor_a[..., None] + weighted_b.reshape(wide) * factor_b[..., None]
    return (highest, totals_a * factor_a + totals_b * factor_b, weighted.reshape(shaped))

def page_partials(group_q, page_rows, row_lengths, key_rows, value_rows, first_page):
    page_count = key_rows.shape[0]
    slot_count = group_q.shape[0]
    head_count = group_q.shape[1] // HEAD_DIM
    page_ids = first_page + jnp.arange(page_count, dtype=jnp.int32)
    table_steps = jnp.arange(page_rows.shape[1], dtype=jnp.int32)
    live_step = (table_steps * PAGE)[None, :] < row_lengths[:, None]
    matches = (page_rows[:, :, None] == page_ids[None, None, :]) & live_step[:, :, None]
    owned_page = jnp.any(matches, axis=1)
    where_at = lax.optimization_barrier(jnp.sum(jnp.where(matches, table_steps[None, :, None], 0), axis=1))
    offsets = jnp.arange(PAGE, dtype=jnp.int32)
    token_pos = where_at[:, :, None] * PAGE + offsets[None, None, :]
    visible = (owned_page[:, :, None] & (token_pos < row_lengths[:, None, None])).reshape(slot_count, page_count * PAGE)
    query_heads = group_q.reshape(slot_count, head_count, HEAD_DIM).astype(jnp.float32)
    key_heads = key_rows.reshape(page_count * PAGE, head_count, HEAD_DIM).astype(jnp.float32)
    value_heads = value_rows.reshape(page_count * PAGE, head_count, HEAD_DIM).astype(jnp.float32)
    scores = jnp.einsum('shd,khd->hsk', query_heads, key_heads) * HEAD_DIM ** (-0.5)
    scores = jnp.where(visible[None], scores, NEG_FILL)
    maxima = lax.optimization_barrier(jnp.max(scores, axis=2))
    exp_terms = jnp.where(visible[None], jnp.exp(scores - maxima[..., None]), 0.0)
    totals = lax.optimization_barrier(jnp.sum(exp_terms, axis=2))
    weights = exp_terms.astype(jnp.bfloat16)
    weighted = jnp.einsum('hsk,khd->shd', weights.astype(jnp.float32), value_heads)
    return (maxima.T, totals.T, weighted.reshape(slot_count, head_count * HEAD_DIM))

def flip_pairs(array):
    return array.reshape((N_GRP // 2, 2) + array.shape[1:])[:, ::-1].reshape(array.shape)

def reference(queries, residual, gain, key_pages, value_pages, page_table, lengths, split_flag, routes, gates, w_gate, w_up, w_down):
    pool_size = PAGES_DEV * N_EP
    group_rows = REQ_DEV * N_EP

    def one_group(inputs):
        group_q, page_rows, row_lengths, key_rows, value_rows = inputs
        return page_partials(group_q, page_rows, row_lengths, key_rows, value_rows, 0)
    maxima, totals, weighted = lax.map(one_group, (queries.reshape(N_GRP, group_rows, D), page_table.reshape(N_GRP, group_rows, LONG_PAGES), lengths.reshape(N_GRP, group_rows), key_pages.reshape(N_GRP, pool_size, PAGE, D), value_pages.reshape(N_GRP, pool_size, PAGE, D)))
    joined = merge_parts((maxima, totals, weighted), (flip_pairs(maxima), flip_pairs(totals), flip_pairs(weighted)))
    is_split = (split_flag.reshape(N_GRP, group_rows) == 1)[..., None]
    totals = jnp.where(is_split, joined[1], totals)
    weighted = jnp.where(is_split, joined[2], weighted)
    attn = (weighted.reshape(N_GRP, group_rows, HEADS, HEAD_DIM) / totals[..., None]).reshape(ROWS, D).astype(jnp.bfloat16)
    stream = residual.astype(jnp.float32) + attn.astype(jnp.float32)
    normed = (stream * lax.rsqrt(lax.optimization_barrier(jnp.mean(stream * stream, axis=-1, keepdims=True)) + NORM_EPS) * gain.astype(jnp.float32)).astype(jnp.bfloat16)
    device_count = N_GRP * N_EP
    expert_count = N_EP
    slot_count = expert_count * CAP
    chosen = routes.reshape(device_count, REQ_DEV * 2)
    one_hot = (chosen[:, :, None] == jnp.arange(expert_count, dtype=jnp.int32)[None, None, :]).astype(jnp.int32)
    ranking = lax.optimization_barrier(jnp.sum((jnp.cumsum(one_hot, axis=1) - one_hot) * one_hot, axis=2))
    slot_of = chosen * CAP + ranking
    slot_ids = jnp.arange(slot_count, dtype=jnp.int32)
    placing = (slot_ids[None, :, None] == slot_of[:, None, :]).astype(jnp.float32)
    doubled = jnp.repeat(normed.reshape(device_count, REQ_DEV, D), 2, axis=1).astype(jnp.float32)
    outgoing = jnp.einsum('dca,dae->dce', placing, doubled).astype(jnp.bfloat16)
    expert_inputs = outgoing.reshape(device_count, expert_count, CAP, D).transpose(1, 0, 2, 3).reshape(expert_count, device_count * CAP, D)

    def expert_out(inputs):
        rows_in, gate_matrix, up_matrix, down_matrix = inputs
        gate_part = jnp.dot(rows_in, gate_matrix, preferred_element_type=jnp.float32)
        up_part = jnp.dot(rows_in, up_matrix, preferred_element_type=jnp.float32)
        inner = (jax.nn.silu(gate_part) * up_part).astype(jnp.bfloat16)
        return jnp.dot(inner, down_matrix, preferred_element_type=jnp.float32).astype(jnp.bfloat16)
    results = lax.map(expert_out, (expert_inputs, w_gate, w_up, w_down))
    returned = results.reshape(expert_count, device_count, CAP, D).transpose(1, 0, 2, 3).reshape(device_count, slot_count, D)
    picking = (slot_of[:, :, None] == slot_ids[None, None, :]).astype(jnp.float32) * gates.reshape(device_count, REQ_DEV * 2)[:, :, None].astype(jnp.float32)
    blending = picking.reshape(device_count, REQ_DEV, 2, slot_count).sum(axis=2).astype(jnp.bfloat16)
    mixture = jnp.einsum('drc,dce->dre', blending.astype(jnp.float32), returned.astype(jnp.float32)).reshape(ROWS, D)
    return (attn.astype(jnp.float32) + mixture).astype(jnp.bfloat16)
```

```python
import functools

import jax
import jax.numpy as jnp
from jax import lax
from jax.experimental import pallas as pl
from jax.experimental.pallas import tpu as pltpu
from jax.sharding import PartitionSpec as P

HEAD_DIM = 64
PAGE = 128
LANES = 128
NEG_FILL = -1e30
NEG_FLOOR = -1e29
NORM_EPS = 1e-06
TOP = 2
B_COLS = 384

F32 = jnp.float32
BF16 = jnp.bfloat16


def iota(shape, axis):
    return lax.broadcasted_iota(jnp.int32, shape, axis)


def dot(a, b, contract=((1,), (0,))):
    return lax.dot_general(a, b, (contract, ((), ())), preferred_element_type=F32)


def fused(
    sizes,
    q_ref, res_ref, gain_ref, pt_ref, routes_ref, gates_ref,
    len_ref, split_ref,
    key_hbm, value_hbm, wg_hbm, wu_hbm, wd_hbm,
    out_ref,
    kbuf, vbuf, wg, wu, wd,
    e_ref, hm_ref, qp_ref, lim_ref, st_ref, w_ref, own_ref, o_ref,
    pw_ref, rs_ref, rt_ref,
    r_all, st_all, a_all, b_send, b_recv, x_all, y_send, y_recv, z_send, z_recv,
    kv_sem, w_sem,
    r_ss, r_rs, st_ss, st_rs, a_ss, a_rs, b_ss, b_rs, x_ss, x_rs, y_ss, y_rs, z_ss, z_rs,
):
    n_grp, n_ep, cap = sizes
    req_dev, D = res_ref.shape
    R = q_ref.shape[0]
    J = pt_ref.shape[1]
    PD = key_hbm.shape[0]
    half = D // 2
    heads = D // HEAD_DIM
    HP = hm_ref.shape[0]
    slots = n_ep * cap
    NPP = own_ref.shape[0]
    n_pages = n_ep * PD

    g = lax.axis_index("grp")
    e = lax.axis_index("ep")
    mate = g + 1 - 2 * lax.rem(g, 2)

    ep_peers = [lax.rem(e + k, n_ep) for k in range(1, n_ep)]
    grp_peers = [lax.rem(g + k, n_grp) for k in range(1, n_grp)]

    barrier = pltpu.get_barrier_semaphore()
    for peer in ep_peers:
        pl.semaphore_signal(barrier, inc=1, device_id=(g, peer), device_id_type=pl.DeviceIdType.MESH)
    for peer in grp_peers:
        pl.semaphore_signal(barrier, inc=1, device_id=(peer, e), device_id_type=pl.DeviceIdType.MESH)
    for peer in ep_peers:
        pl.semaphore_signal(barrier, inc=1, device_id=(mate, peer), device_id_type=pl.DeviceIdType.MESH)

    def kv_copies(p):
        return (
            pltpu.make_async_copy(key_hbm.at[p], kbuf.at[p], kv_sem.at[0, p]),
            pltpu.make_async_copy(value_hbm.at[p], vbuf.at[p], kv_sem.at[1, p]),
        )

    for p in range(PD):
        for copy in kv_copies(p):
            copy.start()
    w_copies = [
        pltpu.make_async_copy(wg_hbm.at[0], wg, w_sem.at[0]),
        pltpu.make_async_copy(wu_hbm.at[0], wu, w_sem.at[1]),
        pltpu.make_async_copy(wd_hbm.at[0], wd, w_sem.at[2]),
    ]
    for copy in w_copies:
        copy.start()

    def remote(src, dst, ss, rs, device):
        return pltpu.make_async_remote_copy(
            src_ref=src, dst_ref=dst, send_sem=ss, recv_sem=rs,
            device_id=device, device_id_type=pl.DeviceIdType.MESH,
        )

    res = res_ref[...].astype(F32)
    r_all[e, 0:req_dev, 0:half] = res[:, :half]
    r_all[e, req_dev:2 * req_dev, 0:half] = res[:, half:]
    route_lane = iota((2 * req_dev, LANES), 1)
    routes = routes_ref[...]
    routes_f = routes.astype(F32)
    r_all[e, :, half:half + LANES] = jnp.zeros((2 * req_dev, LANES), F32)
    r_all[e, 0:req_dev, half:half + LANES] = jnp.where(
        route_lane[:req_dev] == 0, routes_f[:, 0:1],
        jnp.where(route_lane[:req_dev] == 1, routes_f[:, 1:2], 0.0),
    )
    pl.semaphore_wait(barrier, 2 * (n_ep - 1) + n_grp - 1)
    r_sends = [
        remote(r_all.at[e], r_all.at[e], r_ss.at[k], r_rs.at[e], (g, peer))
        for k, peer in enumerate(ep_peers)
    ]
    for copy in r_sends:
        copy.start()

    first_col = iota((LANES, D), 0) * HEAD_DIM
    col = iota((LANES, D), 1)
    in_head = (col >= first_col) & (col < first_col + HEAD_DIM)
    e_ref[...] = jnp.where(in_head, 1.0, 0.0).astype(BF16)
    hm_ref[...] = jnp.where(in_head[:HP], 1.0, 0.0)
    st_ref[...] = jnp.zeros_like(st_ref)
    pw_ref[...] = jnp.zeros_like(pw_ref)

    split_row = 0
    for r in range(R):
        split_row = split_row + jnp.where(split_ref[r] == 1, r, 0)

    page_id = iota((NPP, J), 0)
    j_start = iota((1, J), 1) * PAGE
    local_id = iota((PD, J), 0) + e * PD
    owner = jnp.full((NPP, J), -1.0, F32)
    own_local = jnp.full((PD, J), -1.0, F32)
    limit = jnp.zeros((PD, J), F32)
    length_col = jnp.zeros((R, 1), jnp.int32)
    split_col = jnp.zeros((R, 1), jnp.int32)
    row_col = iota((R, 1), 0)
    for r in range(R):
        length = len_ref[r]
        entries = jnp.where(j_start < length, pt_ref[r:r + 1, :], -1)
        owner = jnp.where(page_id == entries, float(r), owner)
        hit = local_id == entries
        own_local = jnp.where(hit, float(r), own_local)
        limit = jnp.where(hit, jnp.minimum(length - j_start, PAGE).astype(F32), limit)
        length_col = jnp.where(row_col == r, length, length_col)
        split_col = jnp.where(row_col == r, split_ref[r], split_col)
    owner = jnp.max(owner, axis=1, keepdims=True)
    page_col = iota((NPP, LANES), 0)
    mate_pages = (page_col >= n_pages) & (page_col < n_pages + n_ep)
    own_ref[...] = jnp.where(
        mate_pages, split_row.astype(F32), jnp.broadcast_to(owner, (NPP, LANES))
    )
    own_local = jnp.max(own_local, axis=1, keepdims=True)
    limit = jnp.sum(limit, axis=1, keepdims=True)
    lim_ref[...] = jnp.broadcast_to(limit, (PD, LANES))
    split_local = jnp.broadcast_to(own_local, (PD, LANES)) == split_row.astype(F32)

    page_lane = iota((R, NPP), 1)
    o_rows = jnp.where(
        (page_lane >= n_pages) & (page_lane < n_pages + n_ep) & (split_col == 1), 1.0, 0.0
    )
    for j in range(J):
        entry = jnp.where(length_col > j * PAGE, pt_ref[:, j:j + 1], -1)
        o_rows = jnp.where(page_lane == entry, 1.0, o_rows)
    o_ref[...] = o_rows.astype(BF16)

    queries = q_ref[...].astype(F32)
    page_q = jnp.zeros((PD, D), F32)
    for r in range(R):
        page_q = jnp.where(own_local == float(r), queries[r:r + 1, :], page_q)
    qp_ref[...] = page_q

    token = iota((1, LANES), 1).astype(F32)
    stat_lane = iota((HP, LANES), 1)

    def page_step(p):
        for copy in kv_copies(p):
            copy.wait()
        q_page = qp_ref[pl.ds(p, 1), :]
        q_heads = (jnp.broadcast_to(q_page, (HP, D)) * hm_ref[...]).astype(BF16)
        scores = dot(q_heads, kbuf[p], ((1,), (1,))) * HEAD_DIM ** (-0.5)
        visible = token < lim_ref[pl.ds(p, 1), :]
        scores = jnp.where(visible, scores, NEG_FILL)
        top = jnp.maximum(jnp.max(scores, axis=1, keepdims=True), NEG_FLOOR)
        terms = jnp.exp(scores - top)
        total = jnp.sum(terms, axis=1, keepdims=True)
        st_ref[0:HP, :] = jnp.where(stat_lane == p, top, st_ref[0:HP, :])
        st_ref[64:64 + HP, :] = jnp.where(stat_lane == p, total, st_ref[64:64 + HP, :])
        wide = dot(terms.astype(BF16), vbuf[p])
        w_ref[pl.ds(p, 1), :] = jnp.sum(wide * hm_ref[...], axis=0, keepdims=True)

    def pages(i, carry):
        page_step(2 * i)
        page_step(2 * i + 1)
        return carry

    lax.fori_loop(0, PD // 2, pages, 0)

    head_lane = iota((1, LANES), 1) < heads

    weighted = w_ref[...]
    a_all[e] = jnp.concatenate([weighted[:, :half], weighted[:, half:]], axis=0).astype(BF16)
    stats = jnp.transpose(st_ref[...])[0:PD, :]
    st_all[e] = stats
    exchange = []
    for k, peer in enumerate(ep_peers):
        exchange.append(remote(a_all.at[e], a_all.at[e], a_ss.at[k], a_rs.at[e], (g, peer)))
        exchange.append(remote(st_all.at[e], st_all.at[e], st_ss.at[k], st_rs.at[e], (g, peer)))
    for copy in exchange:
        copy.start()

    totals = pltpu.roll(stats, 64, 1)
    split_top = jnp.max(jnp.where(split_local, stats, NEG_FILL), axis=0, keepdims=True)
    factor = jnp.where(split_local & head_lane, jnp.exp(stats - split_top), 0.0)
    split_total = jnp.sum(factor * totals, axis=0, keepdims=True)
    part = jnp.sum(dot(factor.astype(BF16), e_ref[...]) * weighted, axis=0, keepdims=True)
    b_send[...] = jnp.zeros_like(b_send)
    b_rows = D // B_COLS
    for i in range(b_rows):
        b_send[i:i + 1, :] = part[:, i * B_COLS:(i + 1) * B_COLS]
    b_send[b_rows:b_rows + 1, 0:LANES] = split_top
    b_send[b_rows:b_rows + 1, LANES:2 * LANES] = split_total
    b_targets = [e] + ep_peers
    b_sends = [
        remote(b_send, b_recv.at[e], b_ss.at[k], b_rs.at[e], (mate, peer))
        for k, peer in enumerate(b_targets)
    ]
    for copy in b_sends:
        copy.start()

    for src in ep_peers:
        remote(r_all.at[src], r_all.at[src], r_ss.at[0], r_rs.at[src], (g, src)).wait_recv()
    for s in range(n_ep):
        rows = slice(s * req_dev, (s + 1) * req_dev)
        rs_ref[rows, 0:half] = r_all[s, 0:req_dev, 0:half]
        rs_ref[rows, half:D] = r_all[s, req_dev:2 * req_dev, 0:half]
        rt_ref[rows, :] = r_all[s, 0:req_dev, half:half + LANES]

    expert = e.astype(F32)
    chosen = rt_ref[...]
    has_col = jnp.where((chosen[:, 0:1] == expert) | (chosen[:, 1:2] == expert), 1.0, 0.0)
    r_sub = iota((R, R), 0)
    r_lane = iota((R, R), 1)
    has_row = jnp.sum(jnp.where(r_sub == r_lane, has_col, 0.0), axis=0, keepdims=True)
    earlier = (r_sub < r_lane) & (r_sub // req_dev == r_lane // req_dev)
    rank_row = jnp.sum(jnp.where(earlier, has_col, 0.0), axis=0, keepdims=True)
    slot_sub = iota((slots, R), 0)
    slot_row = iota((slots, R), 1)
    pick = jnp.where(
        (slot_sub // cap == slot_row // req_dev)
        & (has_row > 0.5)
        & (rank_row == (slot_sub % cap).astype(F32)),
        1.0, 0.0,
    ).astype(BF16)

    slot_lane = iota((req_dev, LANES), 1)
    first_hit = slot_lane // cap == routes[:, 0:1]
    second_hit = slot_lane // cap == routes[:, 1:2]
    gates = gates_ref[...].astype(F32)
    hits = jnp.where(first_hit | second_hit, 1.0, 0.0)
    row_sub = iota((req_dev, LANES), 0)
    rank = jnp.zeros((req_dev, LANES), F32)
    for i in range(req_dev - 1):
        rank = rank + jnp.where(row_sub > i, hits[i:i + 1, :], 0.0)
    blend = jnp.where(first_hit, gates[:, 0:1], 0.0) + jnp.where(second_hit, gates[:, 1:2], 0.0)
    blend = jnp.where(rank == (slot_lane % cap).astype(F32), blend, 0.0)

    for src in ep_peers:
        remote(st_all.at[src], st_all.at[src], st_ss.at[0], st_rs.at[src], (g, src)).wait_recv()
    for src in b_targets:
        remote(b_send, b_recv.at[src], b_ss.at[0], b_rs.at[src], (mate, src)).wait_recv()
    extra = NPP - n_pages
    extra_sub = iota((extra, LANES), 0)
    extra_top = jnp.full((extra, LANES), NEG_FILL, F32)
    extra_total = jnp.zeros((extra, LANES), F32)
    for s in range(n_ep):
        extra_top = jnp.where(extra_sub == s, b_recv[s, b_rows:b_rows + 1, 0:LANES], extra_top)
        extra_total = jnp.where(
            extra_sub == s, b_recv[s, b_rows:b_rows + 1, LANES:2 * LANES], extra_total
        )
        for i in range(b_rows):
            pw_ref[s:s + 1, i * B_COLS:(i + 1) * B_COLS] = b_recv[s, i:i + 1, :]
    all_stats = st_all[...].reshape(n_pages, LANES)
    all_top = jnp.concatenate([all_stats, extra_top], axis=0)
    all_total = jnp.concatenate([pltpu.roll(all_stats, 64, 1), extra_total], axis=0)
    owners = own_ref[...]
    row_top = jnp.zeros((NPP, LANES), F32)
    for r in range(R):
        mine = owners == float(r)
        highest = jnp.max(jnp.where(mine, all_top, NEG_FILL), axis=0, keepdims=True)
        row_top = jnp.where(mine, highest, row_top)
    owned = (owners >= 0.0) & head_lane
    scale = jnp.where(owned, jnp.exp(jnp.where(owned, all_top - row_top, 0.0)), 0.0)
    scaled_total = scale * all_total
    row_total = jnp.ones((NPP, LANES), F32)
    for r in range(R):
        mine = owners == float(r)
        summed = jnp.sum(jnp.where(mine, scaled_total, 0.0), axis=0, keepdims=True)
        row_total = jnp.where(mine, summed, row_total)
    share = jnp.where(owned, scale / jnp.where(owned, row_total, 1.0), 0.0).astype(BF16)

    for src in ep_peers:
        remote(a_all.at[src], a_all.at[src], a_ss.at[0], a_rs.at[src], (g, src)).wait_recv()
    parts = a_all[...].astype(F32)
    attn = []
    for h in range(2):
        columns = slice(h * half, (h + 1) * half)
        own_pages = parts[:, h * PD:(h + 1) * PD, :].reshape(n_pages, half)
        values = jnp.concatenate([own_pages, pw_ref[:, columns]], axis=0)
        terms = (dot(share, e_ref[:, columns]) * values).astype(BF16)
        attn.append(dot(o_ref[...], terms).astype(BF16))
    stream = [rs_ref[:, h * half:(h + 1) * half] + attn[h].astype(F32) for h in range(2)]
    square = sum(jnp.sum(s * s, axis=1, keepdims=True) for s in stream) * (1.0 / D)
    inverse = lax.rsqrt(square + NORM_EPS)
    normed = [
        (stream[h] * inverse * gain_ref[:, h * half:(h + 1) * half].astype(F32)).astype(BF16)
        for h in range(2)
    ]
    x_all[g] = jnp.concatenate([dot(pick, n) for n in normed], axis=0).astype(BF16)

    x_sends = [
        remote(x_all.at[g], x_all.at[g], x_ss.at[k], x_rs.at[g], (peer, e))
        for k, peer in enumerate(grp_peers)
    ]
    for copy in x_sends:
        copy.start()
    own_pick = jnp.where(iota((req_dev, R), 1) == iota((req_dev, R), 0) + e * req_dev, 1.0, 0.0)
    own_attn = [dot(own_pick.astype(BF16), a) for a in attn]
    for copy in w_copies:
        copy.wait()
    for src in grp_peers:
        remote(x_all.at[src], x_all.at[src], x_ss.at[0], x_rs.at[src], (src, e)).wait_recv()

    rows_in = x_all[...].astype(F32)
    x_lo = rows_in[:, :slots, :].reshape(n_grp * slots, half).astype(BF16)
    x_hi = rows_in[:, slots:, :].reshape(n_grp * slots, half).astype(BF16)
    gate_part = dot(x_lo, wg[0:half, :]) + dot(x_hi, wg[half:D, :])
    up_part = dot(x_lo, wu[0:half, :]) + dot(x_hi, wu[half:D, :])
    inner = (gate_part / (1.0 + jnp.exp(-gate_part)) * up_part).astype(BF16)
    for h in range(2):
        y_half = dot(inner, wd[:, h * half:(h + 1) * half])
        y_send[:, h * slots:(h + 1) * slots, :] = y_half.reshape(n_grp, slots, half).astype(BF16)

    y_sends = [
        remote(y_send.at[peer], y_recv.at[g], y_ss.at[k], y_rs.at[g], (peer, e))
        for k, peer in enumerate(grp_peers)
    ]
    for copy in y_sends:
        copy.start()
    summed = y_send[g].astype(F32)
    for src in grp_peers:
        remote(y_send.at[src], y_recv.at[src], y_ss.at[0], y_rs.at[src], (src, e)).wait_recv()
        summed = summed + y_recv[src].astype(F32)
    summed = summed.astype(BF16).astype(F32)

    for s in range(n_ep):
        z_send[s, 0:cap, :] = summed[s * cap:(s + 1) * cap, :]
        z_send[s, cap:2 * cap, :] = summed[slots + s * cap:slots + (s + 1) * cap, :]
    z_sends = [
        remote(z_send.at[peer], z_recv.at[e], z_ss.at[k], z_rs.at[e], (g, peer))
        for k, peer in enumerate(ep_peers)
    ]
    for copy in z_sends:
        copy.start()
    z_recv[e] = z_send[e]
    for src in ep_peers:
        remote(z_send.at[src], z_recv.at[src], z_ss.at[0], z_rs.at[src], (g, src)).wait_recv()
    for h in range(2):
        update = own_attn[h]
        for s in range(n_ep):
            for c in range(cap):
                slot = s * cap + c
                update = update + blend[:, slot:slot + 1] * z_recv[s, h * cap + c:h * cap + c + 1, :]
        out_ref[:, h * half:(h + 1) * half] = update.astype(BF16)

    for copy in r_sends + exchange + b_sends + x_sends + y_sends + z_sends:
        copy.wait_send()


def on_device(
    n_grp, n_ep,
    queries, residual, gain, key_pages, value_pages, page_table, lengths, split_flag,
    routes, gates, w_gate, w_up, w_down,
):
    req_dev, D = residual.shape
    R = queries.shape[0]
    PD = key_pages.shape[0]
    F = w_gate.shape[2]
    half = D // 2
    heads = D // HEAD_DIM
    HP = -(-heads // 8) * 8
    cap = max(2, (TOP * req_dev + n_ep - 1) // n_ep)
    slots = n_ep * cap
    n_pages = n_ep * PD
    NPP = -(-(n_pages + n_ep) // 16) * 16
    vmem = pl.BlockSpec(memory_space=pltpu.VMEM)
    smem = pl.BlockSpec(memory_space=pltpu.SMEM)
    hbm = pl.BlockSpec(memory_space=pl.ANY)
    dma = pltpu.SemaphoreType.DMA
    scratch = [
        pltpu.VMEM((PD, PAGE, D), BF16),
        pltpu.VMEM((PD, PAGE, D), BF16),
        pltpu.VMEM((D, F), BF16),
        pltpu.VMEM((D, F), BF16),
        pltpu.VMEM((F, D), BF16),
        pltpu.VMEM((LANES, D), BF16),
        pltpu.VMEM((HP, D), F32),
        pltpu.VMEM((PD, D), F32),
        pltpu.VMEM((PD, LANES), F32),
        pltpu.VMEM((LANES, LANES), F32),
        pltpu.VMEM((PD, D), F32),
        pltpu.VMEM((NPP, LANES), F32),
        pltpu.VMEM((R, NPP), BF16),
        pltpu.VMEM((NPP - n_pages, D), F32),
        pltpu.VMEM((R, D), F32),
        pltpu.VMEM((R, LANES), F32),
        pltpu.VMEM((n_ep, 2 * req_dev, half + LANES), F32),
        pltpu.VMEM((n_ep, PD, LANES), F32),
        pltpu.VMEM((n_ep, 2 * PD, half), BF16),
        pltpu.VMEM((8, B_COLS), F32),
        pltpu.VMEM((n_ep, 8, B_COLS), F32),
        pltpu.VMEM((n_grp, 2 * slots, half), BF16),
        pltpu.VMEM((n_grp, 2 * slots, half), BF16),
        pltpu.VMEM((n_grp, 2 * slots, half), BF16),
        pltpu.VMEM((n_ep, 2 * cap, half), F32),
        pltpu.VMEM((n_ep, 2 * cap, half), F32),
        dma((2, PD)),
        dma((3,)),
    ]
    for senders, receivers in (
        (n_ep, n_ep), (n_ep, n_ep), (n_ep, n_ep), (n_ep, n_ep), (n_grp, n_grp), (n_grp, n_grp), (n_ep, n_ep)
    ):
        scratch += [dma((senders,)), dma((receivers,))]
    return pl.pallas_call(
        functools.partial(fused, (n_grp, n_ep, cap)),
        out_shape=jax.ShapeDtypeStruct((req_dev, D), BF16),
        in_specs=[vmem] * 6 + [smem] * 2 + [hbm] * 5,
        out_specs=vmem,
        scratch_shapes=scratch,
        compiler_params=pltpu.CompilerParams(
            collective_id=0, has_side_effects=True, vmem_limit_bytes=56 * 1024 * 1024
        ),
    )(
        queries, residual, gain.reshape(1, D), page_table, routes, gates,
        lengths, split_flag,
        key_pages, value_pages, w_gate, w_up, w_down,
    )


def solution(mesh):
    in_specs = (
        P("grp", None),
        P(("grp", "ep"), None),
        P(),
        P(("grp", "ep"), None, None),
        P(("grp", "ep"), None, None),
        P("grp", None),
        P("grp"),
        P("grp"),
        P(("grp", "ep"), None),
        P(("grp", "ep"), None),
        P("ep", None, "grp"),
        P("ep", None, "grp"),
        P("ep", "grp", None),
    )
    return jax.shard_map(
        functools.partial(on_device, mesh.shape["grp"], mesh.shape["ep"]),
        mesh=mesh, in_specs=in_specs, out_specs=P(("grp", "ep"), None), check_vma=False,
    )
```

```python
import functools

import jax
import jax.numpy as jnp
from jax import lax
from jax.experimental import pallas as pl
from jax.experimental.pallas import tpu as pltpu
from jax.sharding import PartitionSpec as P

HEAD_DIM = 64
PAGE = 128
LANES = 128
NEG_FILL = -1e30
NEG_FLOOR = -1e29
NORM_EPS = 1e-06
TOP = 2
B_COLS = 384
CHUNKS = 3

F32 = jnp.float32
BF16 = jnp.bfloat16


def iota(shape, axis):
    return lax.broadcasted_iota(jnp.int32, shape, axis)


def dot(a, b, contract=((1,), (0,))):
    return lax.dot_general(a, b, (contract, ((), ())), preferred_element_type=F32)


def fused(
    sizes,
    q_ref, res_ref, gain_ref, pt_ref, routes_ref, gates_ref,
    len_ref, split_ref,
    key_hbm, value_hbm, wg_hbm, wu_hbm, wd_hbm,
    out_ref,
    kbuf, vbuf, wg, wu, wd,
    e_ref, hm_ref, qp_ref, lim_ref, st_ref, w_ref, own_ref, o_ref,
    pw_ref, rs_ref, rt_ref,
    r_all, st_all, a_all, b_send, b_recv, x_all, y_send, y_recv, z_send, z_recv,
    kv_sem, w_sem,
    r_ss, r_rs, st_ss, st_rs, a_ss, a_rs, b_ss, b_rs, x_ss, x_rs, y_ss, y_rs, z_ss, z_rs,
):
    n_grp, n_ep, cap = sizes
    req_dev, D = res_ref.shape
    R = q_ref.shape[0]
    J = pt_ref.shape[1]
    PD = key_hbm.shape[0]
    half = D // 2
    heads = D // HEAD_DIM
    HP = hm_ref.shape[0]
    slots = n_ep * cap
    NPP = own_ref.shape[0]
    n_pages = n_ep * PD

    g = lax.axis_index("grp")
    e = lax.axis_index("ep")
    mate = g + 1 - 2 * lax.rem(g, 2)

    ep_peers = [lax.rem(e + k, n_ep) for k in range(1, n_ep)]
    grp_peers = [lax.rem(g + k, n_grp) for k in range(1, n_grp)]

    barrier = pltpu.get_barrier_semaphore()
    for peer in ep_peers:
        pl.semaphore_signal(barrier, inc=1, device_id=(g, peer), device_id_type=pl.DeviceIdType.MESH)
    for peer in grp_peers:
        pl.semaphore_signal(barrier, inc=1, device_id=(peer, e), device_id_type=pl.DeviceIdType.MESH)
    for peer in ep_peers:
        pl.semaphore_signal(barrier, inc=1, device_id=(mate, peer), device_id_type=pl.DeviceIdType.MESH)

    def kv_copies(p):
        return (
            pltpu.make_async_copy(key_hbm.at[p], kbuf.at[p], kv_sem.at[0, p]),
            pltpu.make_async_copy(value_hbm.at[p], vbuf.at[p], kv_sem.at[1, p]),
        )

    for p in range(PD):
        for copy in kv_copies(p):
            copy.start()
    w_copies = [
        pltpu.make_async_copy(wg_hbm.at[0], wg, w_sem.at[0]),
        pltpu.make_async_copy(wu_hbm.at[0], wu, w_sem.at[1]),
        pltpu.make_async_copy(wd_hbm.at[0], wd, w_sem.at[2]),
    ]
    for copy in w_copies:
        copy.start()

    def remote(src, dst, ss, rs, device):
        return pltpu.make_async_remote_copy(
            src_ref=src, dst_ref=dst, send_sem=ss, recv_sem=rs,
            device_id=device, device_id_type=pl.DeviceIdType.MESH,
        )

    res = res_ref[...].astype(F32)
    r_all[e, 0:req_dev, 0:half] = res[:, :half]
    r_all[e, req_dev:2 * req_dev, 0:half] = res[:, half:]
    route_lane = iota((2 * req_dev, LANES), 1)
    eye = iota((req_dev, req_dev), 0) == iota((req_dev, req_dev), 1)

    def column(row):
        return jnp.sum(jnp.where(eye, row, 0.0), axis=1, keepdims=True)

    routes_t = routes_ref[...].astype(F32)
    gates_t = gates_ref[...].astype(F32)
    routes = [column(routes_t[k:k + 1, :]) for k in range(TOP)]
    gates = [column(gates_t[k:k + 1, :]) for k in range(TOP)]
    r_all[e, :, half:half + LANES] = jnp.zeros((2 * req_dev, LANES), F32)
    r_all[e, 0:req_dev, half:half + LANES] = jnp.where(
        route_lane[:req_dev] == 0, routes[0],
        jnp.where(route_lane[:req_dev] == 1, routes[1], 0.0),
    )
    pl.semaphore_wait(barrier, 2 * (n_ep - 1) + n_grp - 1)
    r_sends = [
        remote(r_all.at[e], r_all.at[e], r_ss.at[k], r_rs.at[e], (g, peer))
        for k, peer in enumerate(ep_peers)
    ]
    for copy in r_sends:
        copy.start()

    first_col = iota((LANES, D), 0) * HEAD_DIM
    col = iota((LANES, D), 1)
    in_head = (col >= first_col) & (col < first_col + HEAD_DIM)
    e_ref[...] = jnp.where(in_head, 1.0, 0.0).astype(BF16)
    hm_ref[...] = jnp.where(in_head[:HP], 1.0, 0.0)
    st_ref[...] = jnp.zeros_like(st_ref)
    pw_ref[...] = jnp.zeros_like(pw_ref)

    split_row = 0
    for r in range(R):
        split_row = split_row + jnp.where(split_ref[r] == 1, r, 0)

    page_id = iota((NPP, J), 0)
    j_start = iota((1, J), 1) * PAGE
    local_id = iota((PD, J), 0) + e * PD
    owner = jnp.full((NPP, J), -1.0, F32)
    own_local = jnp.full((PD, J), -1.0, F32)
    limit = jnp.zeros((PD, J), F32)
    length_col = jnp.zeros((R, 1), jnp.int32)
    split_col = jnp.zeros((R, 1), jnp.int32)
    row_col = iota((R, 1), 0)
    for r in range(R):
        length = len_ref[r]
        entries = jnp.where(j_start < length, pt_ref[r:r + 1, :], -1)
        owner = jnp.where(page_id == entries, float(r), owner)
        hit = local_id == entries
        own_local = jnp.where(hit, float(r), own_local)
        limit = jnp.where(hit, jnp.minimum(length - j_start, PAGE).astype(F32), limit)
        length_col = jnp.where(row_col == r, length, length_col)
        split_col = jnp.where(row_col == r, split_ref[r], split_col)
    owner = jnp.max(owner, axis=1, keepdims=True)
    page_col = iota((NPP, LANES), 0)
    mate_pages = (page_col >= n_pages) & (page_col < n_pages + n_ep)
    own_ref[...] = jnp.where(
        mate_pages, split_row.astype(F32), jnp.broadcast_to(owner, (NPP, LANES))
    )
    own_local = jnp.max(own_local, axis=1, keepdims=True)
    limit = jnp.sum(limit, axis=1, keepdims=True)
    lim_ref[...] = jnp.broadcast_to(limit, (PD, LANES))
    split_local = jnp.broadcast_to(own_local, (PD, LANES)) == split_row.astype(F32)

    page_lane = iota((R, NPP), 1)
    o_rows = jnp.where(
        (page_lane >= n_pages) & (page_lane < n_pages + n_ep) & (split_col == 1), 1.0, 0.0
    )
    for j in range(J):
        entry = jnp.where(length_col > j * PAGE, pt_ref[:, j:j + 1], -1)
        o_rows = jnp.where(page_lane == entry, 1.0, o_rows)
    o_ref[...] = o_rows.astype(BF16)

    queries = q_ref[...].astype(F32)
    page_q = jnp.zeros((PD, D), F32)
    for r in range(R):
        page_q = jnp.where(own_local == float(r), queries[r:r + 1, :], page_q)
    qp_ref[...] = page_q

    token = iota((1, LANES), 1).astype(F32)
    stat_lane = iota((HP, LANES), 1)

    def page_step(p):
        for copy in kv_copies(p):
            copy.wait()
        q_page = qp_ref[pl.ds(p, 1), :]
        q_heads = (jnp.broadcast_to(q_page, (HP, D)) * hm_ref[...]).astype(BF16)
        scores = dot(q_heads, kbuf[p], ((1,), (1,))) * HEAD_DIM ** (-0.5)
        visible = token < lim_ref[pl.ds(p, 1), :]
        scores = jnp.where(visible, scores, NEG_FILL)
        top = jnp.maximum(jnp.max(scores, axis=1, keepdims=True), NEG_FLOOR)
        terms = jnp.exp(scores - top)
        total = jnp.sum(terms, axis=1, keepdims=True)
        st_ref[0:HP, :] = jnp.where(stat_lane == p, top, st_ref[0:HP, :])
        st_ref[64:64 + HP, :] = jnp.where(stat_lane == p, total, st_ref[64:64 + HP, :])
        wide = dot(terms.astype(BF16), vbuf[p])
        w_ref[pl.ds(p, 1), :] = jnp.sum(wide * hm_ref[...], axis=0, keepdims=True)

    def pages(i, carry):
        page_step(2 * i)
        page_step(2 * i + 1)
        return carry

    lax.fori_loop(0, PD // 2, pages, 0)

    head_lane = iota((1, LANES), 1) < heads

    weighted = w_ref[...]
    a_all[e] = jnp.concatenate([weighted[:, :half], weighted[:, half:]], axis=0).astype(BF16)
    stats = jnp.transpose(st_ref[...])[0:PD, :]
    st_all[e] = stats
    exchange = []
    for k, peer in enumerate(ep_peers):
        exchange.append(remote(a_all.at[e], a_all.at[e], a_ss.at[k], a_rs.at[e], (g, peer)))
        exchange.append(remote(st_all.at[e], st_all.at[e], st_ss.at[k], st_rs.at[e], (g, peer)))
    for copy in exchange:
        copy.start()

    totals = pltpu.roll(stats, 64, 1)
    split_top = jnp.max(jnp.where(split_local, stats, NEG_FILL), axis=0, keepdims=True)
    factor = jnp.where(split_local & head_lane, jnp.exp(stats - split_top), 0.0)
    split_total = jnp.sum(factor * totals, axis=0, keepdims=True)
    part = jnp.sum(dot(factor.astype(BF16), e_ref[...]) * weighted, axis=0, keepdims=True)
    b_send[...] = jnp.zeros_like(b_send)
    b_rows = D // B_COLS
    for i in range(b_rows):
        b_send[i:i + 1, :] = part[:, i * B_COLS:(i + 1) * B_COLS]
    b_send[b_rows:b_rows + 1, 0:LANES] = split_top
    b_send[b_rows:b_rows + 1, LANES:2 * LANES] = split_total
    b_targets = [e] + ep_peers
    b_sends = [
        remote(b_send, b_recv.at[e], b_ss.at[k], b_rs.at[e], (mate, peer))
        for k, peer in enumerate(b_targets)
    ]
    for copy in b_sends:
        copy.start()

    for src in ep_peers:
        remote(r_all.at[src], r_all.at[src], r_ss.at[0], r_rs.at[src], (g, src)).wait_recv()
    for s in range(n_ep):
        rows = slice(s * req_dev, (s + 1) * req_dev)
        rs_ref[rows, 0:half] = r_all[s, 0:req_dev, 0:half]
        rs_ref[rows, half:D] = r_all[s, req_dev:2 * req_dev, 0:half]
        rt_ref[rows, :] = r_all[s, 0:req_dev, half:half + LANES]

    expert = e.astype(F32)
    chosen = rt_ref[...]
    has_col = jnp.where((chosen[:, 0:1] == expert) | (chosen[:, 1:2] == expert), 1.0, 0.0)
    r_sub = iota((R, R), 0)
    r_lane = iota((R, R), 1)
    has_row = jnp.sum(jnp.where(r_sub == r_lane, has_col, 0.0), axis=0, keepdims=True)
    earlier = (r_sub < r_lane) & (r_sub // req_dev == r_lane // req_dev)
    rank_row = jnp.sum(jnp.where(earlier, has_col, 0.0), axis=0, keepdims=True)
    slot_sub = iota((slots, R), 0)
    slot_row = iota((slots, R), 1)
    pick = jnp.where(
        (slot_sub // cap == slot_row // req_dev)
        & (has_row > 0.5)
        & (rank_row == (slot_sub % cap).astype(F32)),
        1.0, 0.0,
    ).astype(BF16)

    slot_lane = iota((req_dev, LANES), 1)
    slot_expert = (slot_lane // cap).astype(F32)
    first_hit = slot_expert == routes[0]
    second_hit = slot_expert == routes[1]
    hits = jnp.where(first_hit | second_hit, 1.0, 0.0)
    row_sub = iota((req_dev, LANES), 0)
    rank = jnp.zeros((req_dev, LANES), F32)
    for i in range(req_dev - 1):
        rank = rank + jnp.where(row_sub > i, hits[i:i + 1, :], 0.0)
    blend = jnp.where(first_hit, gates[0], 0.0) + jnp.where(second_hit, gates[1], 0.0)
    blend = jnp.where(rank == (slot_lane % cap).astype(F32), blend, 0.0)

    for src in ep_peers:
        remote(st_all.at[src], st_all.at[src], st_ss.at[0], st_rs.at[src], (g, src)).wait_recv()
    for src in b_targets:
        remote(b_send, b_recv.at[src], b_ss.at[0], b_rs.at[src], (mate, src)).wait_recv()
    extra = NPP - n_pages
    extra_sub = iota((extra, LANES), 0)
    extra_top = jnp.full((extra, LANES), NEG_FILL, F32)
    extra_total = jnp.zeros((extra, LANES), F32)
    for s in range(n_ep):
        extra_top = jnp.where(extra_sub == s, b_recv[s, b_rows:b_rows + 1, 0:LANES], extra_top)
        extra_total = jnp.where(
            extra_sub == s, b_recv[s, b_rows:b_rows + 1, LANES:2 * LANES], extra_total
        )
        for i in range(b_rows):
            pw_ref[s:s + 1, i * B_COLS:(i + 1) * B_COLS] = b_recv[s, i:i + 1, :]
    all_stats = st_all[...].reshape(n_pages, LANES)
    all_top = jnp.concatenate([all_stats, extra_top], axis=0)
    all_total = jnp.concatenate([pltpu.roll(all_stats, 64, 1), extra_total], axis=0)
    owners = own_ref[...]
    row_top = jnp.zeros((NPP, LANES), F32)
    for r in range(R):
        mine = owners == float(r)
        highest = jnp.max(jnp.where(mine, all_top, NEG_FILL), axis=0, keepdims=True)
        row_top = jnp.where(mine, highest, row_top)
    owned = (owners >= 0.0) & head_lane
    scale = jnp.where(owned, jnp.exp(jnp.where(owned, all_top - row_top, 0.0)), 0.0)
    scaled_total = scale * all_total
    row_total = jnp.ones((NPP, LANES), F32)
    for r in range(R):
        mine = owners == float(r)
        summed = jnp.sum(jnp.where(mine, scaled_total, 0.0), axis=0, keepdims=True)
        row_total = jnp.where(mine, summed, row_total)
    share = jnp.where(owned, scale / jnp.where(owned, row_total, 1.0), 0.0).astype(BF16)

    for src in ep_peers:
        remote(a_all.at[src], a_all.at[src], a_ss.at[0], a_rs.at[src], (g, src)).wait_recv()
    parts = a_all[...].astype(F32)
    attn = []
    for h in range(2):
        columns = slice(h * half, (h + 1) * half)
        own_pages = parts[:, h * PD:(h + 1) * PD, :].reshape(n_pages, half)
        values = jnp.concatenate([own_pages, pw_ref[:, columns]], axis=0)
        terms = (dot(share, e_ref[:, columns]) * values).astype(BF16)
        attn.append(dot(o_ref[...], terms).astype(BF16))
    stream = [rs_ref[:, h * half:(h + 1) * half] + attn[h].astype(F32) for h in range(2)]
    square = sum(jnp.sum(s * s, axis=1, keepdims=True) for s in stream) * (1.0 / D)
    gain = gain_ref[...].astype(F32).reshape(1, D)
    inverse = lax.rsqrt(square + NORM_EPS)
    normed = [
        (stream[h] * inverse * gain[:, h * half:(h + 1) * half]).astype(BF16)
        for h in range(2)
    ]
    x_all[g] = jnp.concatenate([dot(pick, n) for n in normed], axis=0).astype(BF16)

    x_sends = [
        remote(x_all.at[g], x_all.at[g], x_ss.at[k], x_rs.at[g], (peer, e))
        for k, peer in enumerate(grp_peers)
    ]
    for copy in x_sends:
        copy.start()
    own_pick = jnp.where(iota((req_dev, R), 1) == iota((req_dev, R), 0) + e * req_dev, 1.0, 0.0)
    own_attn = [dot(own_pick.astype(BF16), a) for a in attn]
    for copy in w_copies:
        copy.wait()
    for src in grp_peers:
        remote(x_all.at[src], x_all.at[src], x_ss.at[0], x_rs.at[src], (src, e)).wait_recv()

    rows_in = x_all[...].astype(F32)
    x_lo = rows_in[:, :slots, :].reshape(n_grp * slots, half).astype(BF16)
    x_hi = rows_in[:, slots:, :].reshape(n_grp * slots, half).astype(BF16)
    last = ((1,), (1,))
    gate_part = dot(x_lo, wg[:, 0:half], last) + dot(x_hi, wg[:, half:D], last)
    up_part = dot(x_lo, wu[:, 0:half], last) + dot(x_hi, wu[:, half:D], last)
    inner = (gate_part / (1.0 + jnp.exp(-gate_part)) * up_part).astype(BF16)

    width = D // CHUNKS
    piece = width // 2
    y_sends = []
    for c in range(CHUNKS):
        y_part = dot(inner, wd[:, c * width:(c + 1) * width])
        for h in range(2):
            y_send[c, :, h * slots:(h + 1) * slots, :] = (
                y_part[:, h * piece:(h + 1) * piece].reshape(n_grp, slots, piece).astype(BF16)
            )
        sends = [
            remote(y_send.at[c, peer], y_recv.at[c, g], y_ss.at[c, k], y_rs.at[c, g], (peer, e))
            for k, peer in enumerate(grp_peers)
        ]
        for copy in sends:
            copy.start()
        y_sends += sends

    z_sends = []
    for c in range(CHUNKS):
        summed = y_send[c, g].astype(F32)
        for src in grp_peers:
            remote(
                y_send.at[c, src], y_recv.at[c, src], y_ss.at[c, 0], y_rs.at[c, src], (src, e)
            ).wait_recv()
            summed = summed + y_recv[c, src].astype(F32)
        summed = summed.astype(BF16).astype(F32)
        for s in range(n_ep):
            z_send[c, s, 0:cap, :] = summed[s * cap:(s + 1) * cap, :]
            z_send[c, s, cap:2 * cap, :] = summed[slots + s * cap:slots + (s + 1) * cap, :]
        sends = [
            remote(z_send.at[c, peer], z_recv.at[c, e], z_ss.at[c, k], z_rs.at[c, e], (g, peer))
            for k, peer in enumerate(ep_peers)
        ]
        for copy in sends:
            copy.start()
        z_recv[c, e] = z_send[c, e]
        z_sends += sends
    own_both = jnp.concatenate(own_attn, axis=1)
    for c in range(CHUNKS):
        for src in ep_peers:
            remote(
                z_send.at[c, src], z_recv.at[c, src], z_ss.at[c, 0], z_rs.at[c, src], (g, src)
            ).wait_recv()
        for h in range(2):
            start = c * width + h * piece
            update = own_both[:, start:start + piece]
            for s in range(n_ep):
                for i in range(cap):
                    slot = s * cap + i
                    row = h * cap + i
                    update = update + blend[:, slot:slot + 1] * z_recv[c, s, row:row + 1, :]
            out_ref[:, start:start + piece] = update.astype(BF16)

    for copy in r_sends + exchange + b_sends + x_sends + y_sends + z_sends:
        copy.wait_send()


def on_device(
    n_grp, n_ep,
    queries, residual, gain, key_pages, value_pages, page_table, lengths, split_flag,
    routes, gates, w_gate, w_up, w_down,
):
    req_dev, D = residual.shape
    R = queries.shape[0]
    PD = key_pages.shape[0]
    F = w_gate.shape[2]
    half = D // 2
    heads = D // HEAD_DIM
    HP = -(-heads // 8) * 8
    cap = max(2, (TOP * req_dev + n_ep - 1) // n_ep)
    slots = n_ep * cap
    n_pages = n_ep * PD
    NPP = -(-(n_pages + n_ep) // 16) * 16
    vmem = pl.BlockSpec(memory_space=pltpu.VMEM)
    smem = pl.BlockSpec(memory_space=pltpu.SMEM)
    hbm = pl.BlockSpec(memory_space=pl.ANY)
    dma = pltpu.SemaphoreType.DMA
    scratch = [
        pltpu.VMEM((PD, PAGE, D), BF16),
        pltpu.VMEM((PD, PAGE, D), BF16),
        pltpu.VMEM((F, D), BF16),
        pltpu.VMEM((F, D), BF16),
        pltpu.VMEM((F, D), BF16),
        pltpu.VMEM((LANES, D), BF16),
        pltpu.VMEM((HP, D), F32),
        pltpu.VMEM((PD, D), F32),
        pltpu.VMEM((PD, LANES), F32),
        pltpu.VMEM((LANES, LANES), F32),
        pltpu.VMEM((PD, D), F32),
        pltpu.VMEM((NPP, LANES), F32),
        pltpu.VMEM((R, NPP), BF16),
        pltpu.VMEM((NPP - n_pages, D), F32),
        pltpu.VMEM((R, D), F32),
        pltpu.VMEM((R, LANES), F32),
        pltpu.VMEM((n_ep, 2 * req_dev, half + LANES), F32),
        pltpu.VMEM((n_ep, PD, LANES), F32),
        pltpu.VMEM((n_ep, 2 * PD, half), BF16),
        pltpu.VMEM((8, B_COLS), F32),
        pltpu.VMEM((n_ep, 8, B_COLS), F32),
        pltpu.VMEM((n_grp, 2 * slots, half), BF16),
        pltpu.VMEM((CHUNKS, n_grp, 2 * slots, half // CHUNKS), BF16),
        pltpu.VMEM((CHUNKS, n_grp, 2 * slots, half // CHUNKS), BF16),
        pltpu.VMEM((CHUNKS, n_ep, 2 * cap, half // CHUNKS), F32),
        pltpu.VMEM((CHUNKS, n_ep, 2 * cap, half // CHUNKS), F32),
        dma((2, PD)),
        dma((3,)),
    ]
    for shape in (
        (n_ep,), (n_ep,), (n_ep,), (n_ep,), (n_grp,), (CHUNKS, n_grp), (CHUNKS, n_ep)
    ):
        scratch += [dma(shape), dma(shape)]
    return pl.pallas_call(
        functools.partial(fused, (n_grp, n_ep, cap)),
        out_shape=jax.ShapeDtypeStruct((req_dev, D), BF16),
        in_specs=[vmem] * 6 + [smem] * 2 + [hbm] * 5,
        out_specs=vmem,
        scratch_shapes=scratch,
        compiler_params=pltpu.CompilerParams(
            collective_id=0, has_side_effects=True, vmem_limit_bytes=56 * 1024 * 1024
        ),
    )(
        queries, residual, gain, page_table, routes.T, gates.T,
        lengths, split_flag,
        key_pages, value_pages, jnp.swapaxes(w_gate, 1, 2), jnp.swapaxes(w_up, 1, 2), w_down,
    )


def solution(mesh):
    in_specs = (
        P("grp", None),
        P(("grp", "ep"), None),
        P(),
        P(("grp", "ep"), None, None),
        P(("grp", "ep"), None, None),
        P("grp", None),
        P("grp"),
        P("grp"),
        P(("grp", "ep"), None),
        P(("grp", "ep"), None),
        P("ep", None, "grp"),
        P("ep", None, "grp"),
        P("ep", "grp", None),
    )
    return jax.shard_map(
        functools.partial(on_device, mesh.shape["grp"], mesh.shape["ep"]),
        mesh=mesh, in_specs=in_specs, out_specs=P(("grp", "ep"), None), check_vma=False,
    )
```

```python
import functools

import jax
import jax.numpy as jnp
from jax import lax
from jax.experimental import pallas as pl
from jax.experimental.pallas import tpu as pltpu
from jax.sharding import PartitionSpec as P

HEAD_DIM = 64
PAGE = 128
LANES = 128
NEG_FILL = -1e30
NEG_FLOOR = -1e29
NORM_EPS = 1e-06
TOP = 2
B_COLS = 384
CHUNKS = 3
QUARTERS = ((0, 640), (640, 1280), (1280, 1792), (1792, 2304))
PART_COLS = 640

F32 = jnp.float32
BF16 = jnp.bfloat16


def iota(shape, axis):
    return lax.broadcasted_iota(jnp.int32, shape, axis)


def dot(a, b, contract=((1,), (0,))):
    return lax.dot_general(a, b, (contract, ((), ())), preferred_element_type=F32)


def fused(
    sizes,
    q_ref, res_ref, gain_ref, pt_ref, routes_ref, gates_ref,
    len_ref, split_ref,
    key_hbm, value_hbm, wg_hbm, wu_hbm, wd_hbm,
    out_ref,
    kbuf, vbuf, wg, wu, wd,
    e_ref, hm_ref, qp_ref, lim_ref, st_ref, w_ref, own_ref, o_ref,
    wv_ref, af_ref, rs_ref, rt_ref,
    r_all, st_all, a_all, b_send, b_recv, x_all, y_send, y_pair, y_sum, y_recv, z_send, z_recv,
    kv_sem, w_sem,
    r_ss, r_rs, st_ss, st_rs, a_ss, a_rs, b_ss, b_rs, x_ss, x_rs, p_ss, p_rs, y_ss, y_rs, z_ss, z_rs,
):
    n_grp, n_ep, cap = sizes
    req_dev, D = res_ref.shape
    R = q_ref.shape[0]
    J = pt_ref.shape[1]
    PD = key_hbm.shape[0]
    half = D // 2
    heads = D // HEAD_DIM
    HP = hm_ref.shape[0]
    slots = n_ep * cap
    NPP = own_ref.shape[0]
    n_pages = n_ep * PD

    g = lax.axis_index("grp")
    e = lax.axis_index("ep")
    mate = g + 1 - 2 * lax.rem(g, 2)

    ep_peers = [lax.rem(e + k, n_ep) for k in range(1, n_ep)]
    pairs = n_grp // 2
    side = lax.rem(g, 2)
    pair = lax.div(g, 2)
    pair_peers = [lax.rem(pair + k, pairs) for k in range(1, pairs)]
    mine_first, mate_first = side * pairs, (1 - side) * pairs
    my_place = mine_first + pair

    barrier = pltpu.get_barrier_semaphore()
    for peer in ep_peers:
        pl.semaphore_signal(barrier, inc=1, device_id=(g, peer), device_id_type=pl.DeviceIdType.MESH)
    for peer in pair_peers:
        pl.semaphore_signal(
            barrier, inc=1, device_id=(2 * peer + side, e), device_id_type=pl.DeviceIdType.MESH
        )
    for peer in [e] + ep_peers:
        pl.semaphore_signal(barrier, inc=1, device_id=(mate, peer), device_id_type=pl.DeviceIdType.MESH)

    def kv_copies(p):
        return (
            pltpu.make_async_copy(key_hbm.at[p], kbuf.at[p], kv_sem.at[0, p]),
            pltpu.make_async_copy(value_hbm.at[p], vbuf.at[p], kv_sem.at[1, p]),
        )

    for p in range(PD):
        for copy in kv_copies(p):
            copy.start()
    w_copies = [
        pltpu.make_async_copy(wg_hbm.at[0], wg, w_sem.at[0]),
        pltpu.make_async_copy(wu_hbm.at[0], wu, w_sem.at[1]),
        pltpu.make_async_copy(wd_hbm.at[0], wd, w_sem.at[2]),
    ]

    def remote(src, dst, ss, rs, device):
        return pltpu.make_async_remote_copy(
            src_ref=src, dst_ref=dst, send_sem=ss, recv_sem=rs,
            device_id=device, device_id_type=pl.DeviceIdType.MESH,
        )

    res = res_ref[...].astype(F32)
    r_all[e, 0:req_dev, 0:half] = res[:, :half]
    r_all[e, req_dev:2 * req_dev, 0:half] = res[:, half:]
    route_lane = iota((2 * req_dev, LANES), 1)
    eye = iota((req_dev, req_dev), 0) == iota((req_dev, req_dev), 1)

    def column(row):
        return jnp.sum(jnp.where(eye, row, 0.0), axis=1, keepdims=True)

    routes_t = routes_ref[...].astype(F32)
    gates_t = gates_ref[...].astype(F32)
    routes = [column(routes_t[k:k + 1, :]) for k in range(TOP)]
    gates = [column(gates_t[k:k + 1, :]) for k in range(TOP)]
    r_all[e, :, half:half + LANES] = jnp.zeros((2 * req_dev, LANES), F32)
    r_all[e, 0:req_dev, half:half + LANES] = jnp.where(
        route_lane[:req_dev] == 0, routes[0],
        jnp.where(route_lane[:req_dev] == 1, routes[1], 0.0),
    )
    pl.semaphore_wait(barrier, 2 * n_ep - 1 + pairs - 1)
    r_sends = [
        remote(r_all.at[e], r_all.at[e], r_ss.at[k], r_rs.at[e], (g, peer))
        for k, peer in enumerate(ep_peers)
    ]
    for copy in r_sends:
        copy.start()

    first_col = iota((LANES, D), 0) * HEAD_DIM
    col = iota((LANES, D), 1)
    in_head = (col >= first_col) & (col < first_col + HEAD_DIM)
    e_ref[...] = jnp.where(in_head, 1.0, 0.0).astype(BF16)
    hm_ref[...] = jnp.where(in_head[:HP], 1.0, 0.0)
    st_ref[...] = jnp.zeros_like(st_ref)
    wv_ref[n_pages:, :] = jnp.zeros((NPP - n_pages, D), F32)

    split_row = 0
    for r in range(R):
        split_row = split_row + jnp.where(split_ref[r] == 1, r, 0)

    page_id = iota((NPP, J), 0)
    j_start = iota((1, J), 1) * PAGE
    local_id = iota((PD, J), 0) + e * PD
    owner = jnp.full((NPP, J), -1.0, F32)
    own_local = jnp.full((PD, J), -1.0, F32)
    limit = jnp.zeros((PD, J), F32)
    length_col = jnp.zeros((R, 1), jnp.int32)
    split_col = jnp.zeros((R, 1), jnp.int32)
    row_col = iota((R, 1), 0)
    for r in range(R):
        length = len_ref[r]
        entries = jnp.where(j_start < length, pt_ref[r:r + 1, :], -1)
        owner = jnp.where(page_id == entries, float(r), owner)
        hit = local_id == entries
        own_local = jnp.where(hit, float(r), own_local)
        limit = jnp.where(hit, jnp.minimum(length - j_start, PAGE).astype(F32), limit)
        length_col = jnp.where(row_col == r, length, length_col)
        split_col = jnp.where(row_col == r, split_ref[r], split_col)
    owner = jnp.max(owner, axis=1, keepdims=True)
    page_col = iota((NPP, LANES), 0)
    mate_pages = (page_col >= n_pages) & (page_col < n_pages + n_ep)
    own_ref[...] = jnp.where(
        mate_pages, split_row.astype(F32), jnp.broadcast_to(owner, (NPP, LANES))
    )
    own_local = jnp.max(own_local, axis=1, keepdims=True)
    limit = jnp.sum(limit, axis=1, keepdims=True)
    lim_ref[...] = jnp.broadcast_to(limit, (PD, LANES))
    split_local = jnp.broadcast_to(own_local, (PD, LANES)) == split_row.astype(F32)

    page_lane = iota((R, NPP), 1)
    o_rows = jnp.where(
        (page_lane >= n_pages) & (page_lane < n_pages + n_ep) & (split_col == 1), 1.0, 0.0
    )
    for j in range(J):
        entry = jnp.where(length_col > j * PAGE, pt_ref[:, j:j + 1], -1)
        o_rows = jnp.where(page_lane == entry, 1.0, o_rows)
    o_ref[...] = o_rows.astype(BF16)

    queries = q_ref[...].astype(F32)
    page_q = jnp.zeros((PD, D), F32)
    for r in range(R):
        page_q = jnp.where(own_local == float(r), queries[r:r + 1, :], page_q)
    qp_ref[...] = page_q

    token = iota((1, LANES), 1).astype(F32)
    stat_lane = iota((HP, LANES), 1)

    def page_step(p):
        for copy in kv_copies(p):
            copy.wait()
        q_page = qp_ref[pl.ds(p, 1), :]
        q_heads = (jnp.broadcast_to(q_page, (HP, D)) * hm_ref[...]).astype(BF16)
        scores = dot(q_heads, kbuf[p], ((1,), (1,))) * HEAD_DIM ** (-0.5)
        visible = token < lim_ref[pl.ds(p, 1), :]
        scores = jnp.where(visible, scores, NEG_FILL)
        top = jnp.maximum(jnp.max(scores, axis=1, keepdims=True), NEG_FLOOR)
        terms = jnp.exp(scores - top)
        total = jnp.sum(terms, axis=1, keepdims=True)
        st_ref[0:HP, :] = jnp.where(stat_lane == p, top, st_ref[0:HP, :])
        st_ref[64:64 + HP, :] = jnp.where(stat_lane == p, total, st_ref[64:64 + HP, :])
        wide = dot(terms.astype(BF16), vbuf[p])
        w_ref[pl.ds(p, 1), :] = jnp.sum(wide * hm_ref[...], axis=0, keepdims=True)

    def pages(i, carry):
        page_step(2 * i)
        page_step(2 * i + 1)
        return carry

    part_pages = PD // 2
    af_ref[...] = jnp.zeros_like(af_ref)
    exchange = []

    def send_part(c):
        for i, (low, high) in enumerate(QUARTERS):
            af_ref[i * part_pages:(i + 1) * part_pages, 0:high - low] = (
                w_ref[c * part_pages:(c + 1) * part_pages, low:high]
            )
        a_all[c, e] = af_ref[...].astype(BF16)
        for k, peer in enumerate(ep_peers):
            copy = remote(
                a_all.at[c, e], a_all.at[c, e], a_ss.at[c, k], a_rs.at[c, e], (g, peer)
            )
            copy.start()
            exchange.append(copy)

    lax.fori_loop(0, PD // 4, pages, 0)
    send_part(0)
    lax.fori_loop(PD // 4, PD // 2, pages, 0)
    for copy in w_copies:
        copy.start()
    send_part(1)

    head_lane = iota((1, LANES), 1) < heads

    stats = jnp.transpose(st_ref[...])[0:PD, :]
    st_all[e] = stats
    for k, peer in enumerate(ep_peers):
        copy = remote(st_all.at[e], st_all.at[e], st_ss.at[k], st_rs.at[e], (g, peer))
        copy.start()
        exchange.append(copy)

    totals = pltpu.roll(stats, 64, 1)
    split_top = jnp.max(jnp.where(split_local, stats, NEG_FILL), axis=0, keepdims=True)
    factor = jnp.where(split_local & head_lane, jnp.exp(stats - split_top), 0.0)
    split_total = jnp.sum(factor * totals, axis=0, keepdims=True)
    part = jnp.sum(dot(factor.astype(BF16), e_ref[...]) * w_ref[...], axis=0, keepdims=True)
    b_send[...] = jnp.zeros_like(b_send)
    b_rows = D // B_COLS
    for i in range(b_rows):
        b_send[i:i + 1, :] = part[:, i * B_COLS:(i + 1) * B_COLS]
    b_send[b_rows:b_rows + 1, 0:LANES] = split_top
    b_send[b_rows:b_rows + 1, LANES:2 * LANES] = split_total
    b_targets = [e] + ep_peers
    b_sends = [
        remote(b_send, b_recv.at[e], b_ss.at[k], b_rs.at[e], (mate, peer))
        for k, peer in enumerate(b_targets)
    ]
    for copy in b_sends:
        copy.start()

    for src in ep_peers:
        remote(r_all.at[src], r_all.at[src], r_ss.at[0], r_rs.at[src], (g, src)).wait_recv()
    for s in range(n_ep):
        rows = slice(s * req_dev, (s + 1) * req_dev)
        rs_ref[rows, 0:half] = r_all[s, 0:req_dev, 0:half]
        rs_ref[rows, half:D] = r_all[s, req_dev:2 * req_dev, 0:half]
        rt_ref[rows, :] = r_all[s, 0:req_dev, half:half + LANES]

    expert = e.astype(F32)
    chosen = rt_ref[...]
    has_col = jnp.where((chosen[:, 0:1] == expert) | (chosen[:, 1:2] == expert), 1.0, 0.0)
    r_sub = iota((R, R), 0)
    r_lane = iota((R, R), 1)
    has_row = jnp.sum(jnp.where(r_sub == r_lane, has_col, 0.0), axis=0, keepdims=True)
    earlier = (r_sub < r_lane) & (r_sub // req_dev == r_lane // req_dev)
    rank_row = jnp.sum(jnp.where(earlier, has_col, 0.0), axis=0, keepdims=True)
    slot_sub = iota((slots, R), 0)
    slot_row = iota((slots, R), 1)
    pick = jnp.where(
        (slot_sub // cap == slot_row // req_dev)
        & (has_row > 0.5)
        & (rank_row == (slot_sub % cap).astype(F32)),
        1.0, 0.0,
    ).astype(BF16)

    slot_lane = iota((req_dev, LANES), 1)
    slot_expert = (slot_lane // cap).astype(F32)
    first_hit = slot_expert == routes[0]
    second_hit = slot_expert == routes[1]
    hits = jnp.where(first_hit | second_hit, 1.0, 0.0)
    row_sub = iota((req_dev, LANES), 0)
    rank = jnp.zeros((req_dev, LANES), F32)
    for i in range(req_dev - 1):
        rank = rank + jnp.where(row_sub > i, hits[i:i + 1, :], 0.0)
    blend = jnp.where(first_hit, gates[0], 0.0) + jnp.where(second_hit, gates[1], 0.0)
    blend = jnp.where(rank == (slot_lane % cap).astype(F32), blend, 0.0)

    for src in ep_peers:
        remote(st_all.at[src], st_all.at[src], st_ss.at[0], st_rs.at[src], (g, src)).wait_recv()
    for src in b_targets:
        remote(b_send, b_recv.at[src], b_ss.at[0], b_rs.at[src], (mate, src)).wait_recv()
    extra = NPP - n_pages
    extra_sub = iota((extra, LANES), 0)
    extra_top = jnp.full((extra, LANES), NEG_FILL, F32)
    extra_total = jnp.zeros((extra, LANES), F32)
    for s in range(n_ep):
        extra_top = jnp.where(extra_sub == s, b_recv[s, b_rows:b_rows + 1, 0:LANES], extra_top)
        extra_total = jnp.where(
            extra_sub == s, b_recv[s, b_rows:b_rows + 1, LANES:2 * LANES], extra_total
        )
        for i in range(b_rows):
            row = n_pages + s
            wv_ref[row:row + 1, i * B_COLS:(i + 1) * B_COLS] = b_recv[s, i:i + 1, :]
    all_stats = st_all[...].reshape(n_pages, LANES)
    all_top = jnp.concatenate([all_stats, extra_top], axis=0)
    all_total = jnp.concatenate([pltpu.roll(all_stats, 64, 1), extra_total], axis=0)
    owners = own_ref[...]
    row_top = jnp.zeros((NPP, LANES), F32)
    for r in range(R):
        mine = owners == float(r)
        highest = jnp.max(jnp.where(mine, all_top, NEG_FILL), axis=0, keepdims=True)
        row_top = jnp.where(mine, highest, row_top)
    owned = (owners >= 0.0) & head_lane
    scale = jnp.where(owned, jnp.exp(jnp.where(owned, all_top - row_top, 0.0)), 0.0)
    scaled_total = scale * all_total
    row_total = jnp.ones((NPP, LANES), F32)
    for r in range(R):
        mine = owners == float(r)
        summed = jnp.sum(jnp.where(mine, scaled_total, 0.0), axis=0, keepdims=True)
        row_total = jnp.where(mine, summed, row_total)
    share = jnp.where(owned, scale / jnp.where(owned, row_total, 1.0), 0.0).astype(BF16)

    for c in range(2):
        for src in ep_peers:
            remote(
                a_all.at[c, src], a_all.at[c, src], a_ss.at[c, 0], a_rs.at[c, src], (g, src)
            ).wait_recv()
        for s in range(n_ep):
            arrived = a_all[c, s].astype(F32)
            first = s * PD + c * part_pages
            for i, (low, high) in enumerate(QUARTERS):
                wv_ref[first:first + part_pages, low:high] = (
                    arrived[i * part_pages:(i + 1) * part_pages, 0:high - low]
                )
    attn = []
    for h in range(2):
        columns = slice(h * half, (h + 1) * half)
        terms = (dot(share, e_ref[:, columns]) * wv_ref[:, columns]).astype(BF16)
        attn.append(dot(o_ref[...], terms).astype(BF16))
    stream = [rs_ref[:, h * half:(h + 1) * half] + attn[h].astype(F32) for h in range(2)]
    square = sum(jnp.sum(s * s, axis=1, keepdims=True) for s in stream) * (1.0 / D)
    gain = gain_ref[...].astype(F32).reshape(1, D)
    inverse = lax.rsqrt(square + NORM_EPS)
    normed = [
        (stream[h] * inverse * gain[:, h * half:(h + 1) * half]).astype(BF16)
        for h in range(2)
    ]
    x_all[my_place] = jnp.concatenate([dot(pick, n) for n in normed], axis=0).astype(BF16)

    def x_copy(place, k, device):
        return remote(x_all.at[place], x_all.at[place], x_ss.at[k], x_rs.at[place], device)

    x_sends = [
        x_copy(my_place, k, (2 * peer + side, e)) for k, peer in enumerate(pair_peers)
    ]
    x_sends.append(x_copy(my_place, pairs - 1, (mate, e)))
    for copy in x_sends:
        copy.start()
    own_pick = jnp.where(iota((req_dev, R), 1) == iota((req_dev, R), 0) + e * req_dev, 1.0, 0.0)
    own_attn = [dot(own_pick.astype(BF16), a) for a in attn]
    for k, peer in enumerate(pair_peers):
        x_copy(mine_first + peer, 0, (mate, e)).wait_recv()
        forward = x_copy(mine_first + peer, pairs + k, (mate, e))
        forward.start()
        x_sends.append(forward)
    for copy in w_copies:
        copy.wait()
    for peer in [pair] + pair_peers:
        x_copy(mate_first + peer, 0, (mate, e)).wait_recv()

    rows_in = x_all[...].astype(F32)
    x_lo = rows_in[:, :slots, :].reshape(n_grp * slots, half).astype(BF16)
    x_hi = rows_in[:, slots:, :].reshape(n_grp * slots, half).astype(BF16)
    last = ((1,), (1,))
    gate_part = dot(x_lo, wg[:, 0:half], last) + dot(x_hi, wg[:, half:D], last)
    up_part = dot(x_lo, wu[:, 0:half], last) + dot(x_hi, wu[:, half:D], last)
    inner = (gate_part / (1.0 + jnp.exp(-gate_part)) * up_part).astype(BF16)

    width = D // CHUNKS
    piece = width // 2
    y_sends = []

    def pair_copy(c):
        return remote(
            y_send.at[c, pl.ds(mate_first, pairs)], y_pair.at[c], p_ss.at[c], p_rs.at[c], (mate, e)
        )

    def pair_sum(c):
        pair_copy(c).wait_recv()
        both = y_send[c, pl.ds(mine_first, pairs)].astype(F32) + y_pair[c].astype(F32)
        y_sum[c] = both.astype(BF16)
        for k, peer in enumerate(pair_peers):
            copy = remote(
                y_sum.at[c, peer], y_recv.at[c, pair], y_ss.at[c, k], y_rs.at[c, pair],
                (2 * peer + side, e),
            )
            copy.start()
            y_sends.append(copy)

    for c in range(CHUNKS):
        y_part = dot(inner, wd[:, c * width:(c + 1) * width])
        for h in range(2):
            y_send[c, :, h * slots:(h + 1) * slots, :] = (
                y_part[:, h * piece:(h + 1) * piece].reshape(n_grp, slots, piece).astype(BF16)
            )
        copy = pair_copy(c)
        copy.start()
        y_sends.append(copy)
        if c:
            pair_sum(c - 1)
    pair_sum(CHUNKS - 1)

    z_sends = []
    for c in range(CHUNKS):
        summed = y_sum[c, pair].astype(F32)
        for src in pair_peers:
            remote(
                y_sum.at[c, src], y_recv.at[c, src], y_ss.at[c, 0], y_rs.at[c, src],
                (2 * src + side, e),
            ).wait_recv()
            summed = summed + y_recv[c, src].astype(F32)
        summed = summed.astype(BF16).astype(F32)
        for s in range(n_ep):
            z_send[c, s, 0:cap, :] = summed[s * cap:(s + 1) * cap, :]
            z_send[c, s, cap:2 * cap, :] = summed[slots + s * cap:slots + (s + 1) * cap, :]
        sends = [
            remote(z_send.at[c, peer], z_recv.at[c, e], z_ss.at[c, k], z_rs.at[c, e], (g, peer))
            for k, peer in enumerate(ep_peers)
        ]
        for copy in sends:
            copy.start()
        z_recv[c, e] = z_send[c, e]
        z_sends += sends
    own_both = jnp.concatenate(own_attn, axis=1)
    for c in range(CHUNKS):
        for src in ep_peers:
            remote(
                z_send.at[c, src], z_recv.at[c, src], z_ss.at[c, 0], z_rs.at[c, src], (g, src)
            ).wait_recv()
        for h in range(2):
            start = c * width + h * piece
            update = own_both[:, start:start + piece]
            for s in range(n_ep):
                for i in range(cap):
                    slot = s * cap + i
                    row = h * cap + i
                    update = update + blend[:, slot:slot + 1] * z_recv[c, s, row:row + 1, :]
            out_ref[:, start:start + piece] = update.astype(BF16)

    for copy in r_sends + exchange + b_sends + x_sends + y_sends + z_sends:
        copy.wait_send()


def on_device(
    n_grp, n_ep,
    queries, residual, gain, key_pages, value_pages, page_table, lengths, split_flag,
    routes, gates, w_gate, w_up, w_down,
):
    req_dev, D = residual.shape
    R = queries.shape[0]
    PD = key_pages.shape[0]
    F = w_gate.shape[2]
    half = D // 2
    heads = D // HEAD_DIM
    HP = -(-heads // 8) * 8
    cap = max(2, (TOP * req_dev + n_ep - 1) // n_ep)
    slots = n_ep * cap
    n_pages = n_ep * PD
    NPP = -(-(n_pages + n_ep) // 16) * 16
    vmem = pl.BlockSpec(memory_space=pltpu.VMEM)
    smem = pl.BlockSpec(memory_space=pltpu.SMEM)
    hbm = pl.BlockSpec(memory_space=pl.ANY)
    dma = pltpu.SemaphoreType.DMA
    scratch = [
        pltpu.VMEM((PD, PAGE, D), BF16),
        pltpu.VMEM((PD, PAGE, D), BF16),
        pltpu.VMEM((F, D), BF16),
        pltpu.VMEM((F, D), BF16),
        pltpu.VMEM((F, D), BF16),
        pltpu.VMEM((LANES, D), BF16),
        pltpu.VMEM((HP, D), F32),
        pltpu.VMEM((PD, D), F32),
        pltpu.VMEM((PD, LANES), F32),
        pltpu.VMEM((LANES, LANES), F32),
        pltpu.VMEM((PD, D), F32),
        pltpu.VMEM((NPP, LANES), F32),
        pltpu.VMEM((R, NPP), BF16),
        pltpu.VMEM((NPP, D), F32),
        pltpu.VMEM((2 * PD, PART_COLS), F32),
        pltpu.VMEM((R, D), F32),
        pltpu.VMEM((R, LANES), F32),
        pltpu.VMEM((n_ep, 2 * req_dev, half + LANES), F32),
        pltpu.VMEM((n_ep, PD, LANES), F32),
        pltpu.VMEM((2, n_ep, 2 * PD, PART_COLS), BF16),
        pltpu.VMEM((8, B_COLS), F32),
        pltpu.VMEM((n_ep, 8, B_COLS), F32),
        pltpu.VMEM((n_grp, 2 * slots, half), BF16),
        pltpu.VMEM((CHUNKS, n_grp, 2 * slots, half // CHUNKS), BF16),
        pltpu.VMEM((CHUNKS, n_grp // 2, 2 * slots, half // CHUNKS), BF16),
        pltpu.VMEM((CHUNKS, n_grp // 2, 2 * slots, half // CHUNKS), BF16),
        pltpu.VMEM((CHUNKS, n_grp // 2, 2 * slots, half // CHUNKS), BF16),
        pltpu.VMEM((CHUNKS, n_ep, 2 * cap, half // CHUNKS), F32),
        pltpu.VMEM((CHUNKS, n_ep, 2 * cap, half // CHUNKS), F32),
        dma((2, PD)),
        dma((3,)),
    ]
    for shape in (
        (n_ep,), (n_ep,), (2, n_ep), (n_ep,), (n_grp,), (CHUNKS,), (CHUNKS, n_grp // 2),
        (CHUNKS, n_ep),
    ):
        scratch += [dma(shape), dma(shape)]
    return pl.pallas_call(
        functools.partial(fused, (n_grp, n_ep, cap)),
        out_shape=jax.ShapeDtypeStruct((req_dev, D), BF16),
        in_specs=[vmem] * 6 + [smem] * 2 + [hbm] * 5,
        out_specs=vmem,
        scratch_shapes=scratch,
        compiler_params=pltpu.CompilerParams(
            collective_id=0, has_side_effects=True, vmem_limit_bytes=56 * 1024 * 1024
        ),
    )(
        queries, residual, gain, page_table, routes.T, gates.T,
        lengths, split_flag,
        key_pages, value_pages, jnp.swapaxes(w_gate, 1, 2), jnp.swapaxes(w_up, 1, 2), w_down,
    )


def solution(mesh):
    in_specs = (
        P("grp", None),
        P(("grp", "ep"), None),
        P(),
        P(("grp", "ep"), None, None),
        P(("grp", "ep"), None, None),
        P("grp", None),
        P("grp"),
        P("grp"),
        P(("grp", "ep"), None),
        P(("grp", "ep"), None),
        P("ep", None, "grp"),
        P("ep", None, "grp"),
        P("ep", "grp", None),
    )
    return jax.shard_map(
        functools.partial(on_device, mesh.shape["grp"], mesh.shape["ep"]),
        mesh=mesh, in_specs=in_specs, out_specs=P(("grp", "ep"), None), check_vma=False,
    )
```

```python
import functools

import jax
import jax.numpy as jnp
from jax import lax
from jax.experimental import pallas as pl
from jax.experimental.pallas import tpu as pltpu
from jax.sharding import PartitionSpec as P

HEAD_DIM = 64
PAGE = 128
LANES = 128
NEG_FILL = -1e30
NEG_FLOOR = -1e29
NORM_EPS = 1e-06
TOP = 2
B_COLS = 384
CHUNKS = 3
OCTET = 8
QUARTERS = ((0, 640), (640, 1280), (1280, 1792), (1792, 2304))
PART_COLS = 640

F32 = jnp.float32
BF16 = jnp.bfloat16


def iota(shape, axis):
    return lax.broadcasted_iota(jnp.int32, shape, axis)


def dot(a, b, contract=((1,), (0,))):
    return lax.dot_general(a, b, (contract, ((), ())), preferred_element_type=F32)


def fused(
    sizes,
    q_ref, res_ref, gain_ref, pt_ref, routes_ref, gates_ref,
    len_ref, split_ref,
    key_hbm, value_hbm, wg_hbm, wu_hbm, wd_hbm,
    out_ref,
    kbuf, vbuf, wg, wu, wd,
    e_ref, qp_ref, lim_ref, st_ref, w_ref, own_ref, o_ref,
    wv_ref, af_ref, rs_ref, rt_ref,
    r_all, st_all, a_all, b_send, b_recv, x_all, y_send, y_pair, y_sum, y_recv, z_send, z_recv,
    kv_sem, w_sem,
    r_ss, r_rs, st_ss, st_rs, a_ss, a_rs, b_ss, b_rs, x_ss, x_rs, p_ss, p_rs, y_ss, y_rs, z_ss, z_rs,
):
    n_grp, n_ep, cap = sizes
    req_dev, D = res_ref.shape
    R = q_ref.shape[0]
    J = pt_ref.shape[1]
    PD = key_hbm.shape[0]
    half = D // 2
    heads = D // HEAD_DIM
    HP = -(-heads // OCTET) * OCTET
    slots = n_ep * cap
    NPP = own_ref.shape[0]
    n_pages = n_ep * PD

    g = lax.axis_index("grp")
    e = lax.axis_index("ep")
    mate = g + 1 - 2 * lax.rem(g, 2)

    ep_peers = [lax.rem(e + k, n_ep) for k in range(1, n_ep)]
    pairs = n_grp // 2
    side = lax.rem(g, 2)
    pair = lax.div(g, 2)
    pair_peers = [lax.rem(pair + k, pairs) for k in range(1, pairs)]
    mine_first, mate_first = side * pairs, (1 - side) * pairs
    my_place = mine_first + pair

    barrier = pltpu.get_barrier_semaphore()
    for peer in ep_peers:
        pl.semaphore_signal(barrier, inc=1, device_id=(g, peer), device_id_type=pl.DeviceIdType.MESH)
    for peer in pair_peers:
        pl.semaphore_signal(
            barrier, inc=1, device_id=(2 * peer + side, e), device_id_type=pl.DeviceIdType.MESH
        )
    for peer in [e] + ep_peers:
        pl.semaphore_signal(barrier, inc=1, device_id=(mate, peer), device_id_type=pl.DeviceIdType.MESH)

    def kv_copy(p, which):
        source, held = ((key_hbm, kbuf), (value_hbm, vbuf))[which]
        return pltpu.make_async_copy(source.at[p], held.at[p], kv_sem.at[which, p])

    part_pages = PD // 2
    for c in range(2):
        for which in range(2):
            for p in range(c * part_pages, (c + 1) * part_pages):
                kv_copy(p, which).start()
    w_copies = [
        pltpu.make_async_copy(wg_hbm.at[0], wg, w_sem.at[0]),
        pltpu.make_async_copy(wu_hbm.at[0], wu, w_sem.at[1]),
        pltpu.make_async_copy(wd_hbm.at[0], wd, w_sem.at[2]),
    ]

    def remote(src, dst, ss, rs, device):
        return pltpu.make_async_remote_copy(
            src_ref=src, dst_ref=dst, send_sem=ss, recv_sem=rs,
            device_id=device, device_id_type=pl.DeviceIdType.MESH,
        )

    res = res_ref[...].astype(F32)
    r_all[e, 0:req_dev, 0:half] = res[:, :half]
    r_all[e, req_dev:2 * req_dev, 0:half] = res[:, half:]
    route_lane = iota((2 * req_dev, LANES), 1)
    eye = iota((req_dev, req_dev), 0) == iota((req_dev, req_dev), 1)

    def column(row):
        return jnp.sum(jnp.where(eye, row, 0.0), axis=1, keepdims=True)

    routes_t = routes_ref[...].astype(F32)
    gates_t = gates_ref[...].astype(F32)
    routes = [column(routes_t[k:k + 1, :]) for k in range(TOP)]
    gates = [column(gates_t[k:k + 1, :]) for k in range(TOP)]
    r_all[e, :, half:half + LANES] = jnp.zeros((2 * req_dev, LANES), F32)
    r_all[e, 0:req_dev, half:half + LANES] = jnp.where(
        route_lane[:req_dev] == 0, routes[0],
        jnp.where(route_lane[:req_dev] == 1, routes[1], 0.0),
    )
    first_col = iota((LANES, D), 0) * HEAD_DIM
    col = iota((LANES, D), 1)
    in_head = (col >= first_col) & (col < first_col + HEAD_DIM)
    e_ref[...] = jnp.where(in_head, 1.0, 0.0).astype(BF16)
    st_ref[...] = jnp.zeros_like(st_ref)
    head_mask = jnp.where(in_head[:OCTET, :OCTET * HEAD_DIM], 1.0, 0.0)
    wv_ref[n_pages:, :] = jnp.zeros((NPP - n_pages, D), F32)

    split_row = 0
    for r in range(R):
        split_row = split_row + jnp.where(split_ref[r] == 1, r, 0)

    page_id = iota((NPP, J), 0)
    j_start = iota((1, J), 1) * PAGE
    local_id = iota((PD, J), 0) + e * PD
    owner = jnp.full((NPP, J), -1.0, F32)
    own_local = jnp.full((PD, J), -1.0, F32)
    limit = jnp.zeros((PD, J), F32)
    length_col = jnp.zeros((R, 1), jnp.int32)
    split_col = jnp.zeros((R, 1), jnp.int32)
    row_col = iota((R, 1), 0)
    for r in range(R):
        length = len_ref[r]
        entries = jnp.where(j_start < length, pt_ref[r:r + 1, :], -1)
        owner = jnp.where(page_id == entries, float(r), owner)
        hit = local_id == entries
        own_local = jnp.where(hit, float(r), own_local)
        limit = jnp.where(hit, jnp.minimum(length - j_start, PAGE).astype(F32), limit)
        length_col = jnp.where(row_col == r, length, length_col)
        split_col = jnp.where(row_col == r, split_ref[r], split_col)
    owner = jnp.max(owner, axis=1, keepdims=True)
    page_col = iota((NPP, LANES), 0)
    mate_pages = (page_col >= n_pages) & (page_col < n_pages + n_ep)
    own_ref[...] = jnp.where(
        mate_pages, split_row.astype(F32), jnp.broadcast_to(owner, (NPP, LANES))
    )
    own_local = jnp.max(own_local, axis=1, keepdims=True)
    limit = jnp.sum(limit, axis=1, keepdims=True)
    lim_ref[...] = jnp.broadcast_to(limit, (PD, LANES))
    split_local = jnp.broadcast_to(own_local, (PD, LANES)) == split_row.astype(F32)

    page_lane = iota((R, NPP), 1)
    o_rows = jnp.where(
        (page_lane >= n_pages) & (page_lane < n_pages + n_ep) & (split_col == 1), 1.0, 0.0
    )
    for j in range(J):
        entry = jnp.where(length_col > j * PAGE, pt_ref[:, j:j + 1], -1)
        o_rows = jnp.where(page_lane == entry, 1.0, o_rows)
    o_ref[...] = o_rows.astype(BF16)

    queries = q_ref[...].astype(F32)
    page_q = jnp.zeros((PD, D), F32)
    for r in range(R):
        page_q = jnp.where(own_local == float(r), queries[r:r + 1, :], page_q)
    qp_ref[...] = page_q

    token = iota((1, LANES), 1).astype(F32)
    stat_lane = iota((HP, LANES), 1)
    octets = [
        (i, i * OCTET * HEAD_DIM, min(D, (i + 1) * OCTET * HEAD_DIM)) for i in range(HP // OCTET)
    ]
    af_ref[...] = jnp.zeros_like(af_ref)

    def part(c):
        first = c * part_pages
        for p in range(first, first + part_pages):
            kv_copy(p, 0).wait()
        scores = []
        for p in range(first, first + part_pages):
            rows = []
            for _, low, high in octets:
                q_part = jnp.broadcast_to(qp_ref[p:p + 1, low:high], (OCTET, high - low))
                q_part = (q_part * head_mask[:, :high - low]).astype(BF16)
                rows.append(dot(q_part, kbuf[p, :, low:high], ((1,), (1,))))
            visible = token < lim_ref[p:p + 1, :]
            scores.append(
                jnp.where(visible, jnp.concatenate(rows, axis=0) * HEAD_DIM ** (-0.5), NEG_FILL)
            )
        scores = jnp.concatenate(scores, axis=0)
        top = jnp.maximum(jnp.max(scores, axis=1, keepdims=True), NEG_FLOOR)
        terms = jnp.exp(scores - top)
        total = jnp.sum(terms, axis=1, keepdims=True)
        tops, totals = st_ref[0:HP, :], st_ref[64:64 + HP, :]
        for i in range(part_pages):
            here = stat_lane == first + i
            tops = jnp.where(here, top[i * HP:(i + 1) * HP], tops)
            totals = jnp.where(here, total[i * HP:(i + 1) * HP], totals)
        st_ref[0:HP, :] = tops
        st_ref[64:64 + HP, :] = totals
        for p in range(first, first + part_pages):
            kv_copy(p, 1).wait()
        if c:
            for copy in w_copies:
                copy.start()
        for i in range(part_pages):
            p = first + i
            for o, low, high in octets:
                start = i * HP + o * OCTET
                wide = dot(terms[start:start + OCTET].astype(BF16), vbuf[p, :, low:high])
                w_ref[p:p + 1, low:high] = jnp.sum(
                    wide * head_mask[:, :high - low], axis=0, keepdims=True
                )
        for i, (low, high) in enumerate(QUARTERS):
            af_ref[i * part_pages:(i + 1) * part_pages, 0:high - low] = (
                w_ref[first:first + part_pages, low:high]
            )
        a_all[c, e] = af_ref[...].astype(BF16)

    exchange = []

    def send_part(c):
        for k, peer in enumerate(ep_peers):
            copy = remote(
                a_all.at[c, e], a_all.at[c, e], a_ss.at[c, k], a_rs.at[c, e], (g, peer)
            )
            copy.start()
            exchange.append(copy)

    part(0)
    pl.semaphore_wait(barrier, 2 * n_ep - 1 + pairs - 1)
    r_sends = [
        remote(r_all.at[e], r_all.at[e], r_ss.at[k], r_rs.at[e], (g, peer))
        for k, peer in enumerate(ep_peers)
    ]
    for copy in r_sends:
        copy.start()
    send_part(0)
    part(1)
    send_part(1)

    head_lane = iota((1, LANES), 1) < heads

    stats = jnp.transpose(st_ref[...])[0:PD, :]
    st_all[e] = stats
    for k, peer in enumerate(ep_peers):
        copy = remote(st_all.at[e], st_all.at[e], st_ss.at[k], st_rs.at[e], (g, peer))
        copy.start()
        exchange.append(copy)

    totals = pltpu.roll(stats, 64, 1)
    split_top = jnp.max(jnp.where(split_local, stats, NEG_FILL), axis=0, keepdims=True)
    factor = jnp.where(split_local & head_lane, jnp.exp(stats - split_top), 0.0)
    split_total = jnp.sum(factor * totals, axis=0, keepdims=True)
    split_part = jnp.sum(dot(factor.astype(BF16), e_ref[...]) * w_ref[...], axis=0, keepdims=True)
    b_send[...] = jnp.zeros_like(b_send)
    b_rows = D // B_COLS
    for i in range(b_rows):
        b_send[i:i + 1, :] = split_part[:, i * B_COLS:(i + 1) * B_COLS]
    b_send[b_rows:b_rows + 1, 0:LANES] = split_top
    b_send[b_rows:b_rows + 1, LANES:2 * LANES] = split_total
    b_targets = [e] + ep_peers
    b_sends = [
        remote(b_send, b_recv.at[e], b_ss.at[k], b_rs.at[e], (mate, peer))
        for k, peer in enumerate(b_targets)
    ]
    for copy in b_sends:
        copy.start()

    for src in ep_peers:
        remote(r_all.at[src], r_all.at[src], r_ss.at[0], r_rs.at[src], (g, src)).wait_recv()
    for s in range(n_ep):
        rows = slice(s * req_dev, (s + 1) * req_dev)
        rs_ref[rows, 0:half] = r_all[s, 0:req_dev, 0:half]
        rs_ref[rows, half:D] = r_all[s, req_dev:2 * req_dev, 0:half]
        rt_ref[rows, :] = r_all[s, 0:req_dev, half:half + LANES]

    expert = e.astype(F32)
    chosen = rt_ref[...]
    has_col = jnp.where((chosen[:, 0:1] == expert) | (chosen[:, 1:2] == expert), 1.0, 0.0)
    r_sub = iota((R, R), 0)
    r_lane = iota((R, R), 1)
    has_row = jnp.sum(jnp.where(r_sub == r_lane, has_col, 0.0), axis=0, keepdims=True)
    earlier = (r_sub < r_lane) & (r_sub // req_dev == r_lane // req_dev)
    rank_row = jnp.sum(jnp.where(earlier, has_col, 0.0), axis=0, keepdims=True)
    slot_sub = iota((slots, R), 0)
    slot_row = iota((slots, R), 1)
    pick = jnp.where(
        (slot_sub // cap == slot_row // req_dev)
        & (has_row > 0.5)
        & (rank_row == (slot_sub % cap).astype(F32)),
        1.0, 0.0,
    ).astype(BF16)

    slot_lane = iota((req_dev, LANES), 1)
    slot_expert = (slot_lane // cap).astype(F32)
    first_hit = slot_expert == routes[0]
    second_hit = slot_expert == routes[1]
    hits = jnp.where(first_hit | second_hit, 1.0, 0.0)
    row_sub = iota((req_dev, LANES), 0)
    rank = jnp.zeros((req_dev, LANES), F32)
    for i in range(req_dev - 1):
        rank = rank + jnp.where(row_sub > i, hits[i:i + 1, :], 0.0)
    blend = jnp.where(first_hit, gates[0], 0.0) + jnp.where(second_hit, gates[1], 0.0)
    blend = jnp.where(rank == (slot_lane % cap).astype(F32), blend, 0.0)

    for src in ep_peers:
        remote(st_all.at[src], st_all.at[src], st_ss.at[0], st_rs.at[src], (g, src)).wait_recv()
    for src in b_targets:
        remote(b_send, b_recv.at[src], b_ss.at[0], b_rs.at[src], (mate, src)).wait_recv()
    extra = NPP - n_pages
    extra_sub = iota((extra, LANES), 0)
    extra_top = jnp.full((extra, LANES), NEG_FILL, F32)
    extra_total = jnp.zeros((extra, LANES), F32)
    for s in range(n_ep):
        extra_top = jnp.where(extra_sub == s, b_recv[s, b_rows:b_rows + 1, 0:LANES], extra_top)
        extra_total = jnp.where(
            extra_sub == s, b_recv[s, b_rows:b_rows + 1, LANES:2 * LANES], extra_total
        )
        for i in range(b_rows):
            row = n_pages + s
            wv_ref[row:row + 1, i * B_COLS:(i + 1) * B_COLS] = b_recv[s, i:i + 1, :]
    all_stats = st_all[...].reshape(n_pages, LANES)
    all_top = jnp.concatenate([all_stats, extra_top], axis=0)
    all_total = jnp.concatenate([pltpu.roll(all_stats, 64, 1), extra_total], axis=0)
    owners = own_ref[...]
    row_top = jnp.zeros((NPP, LANES), F32)
    for r in range(R):
        mine = owners == float(r)
        highest = jnp.max(jnp.where(mine, all_top, NEG_FILL), axis=0, keepdims=True)
        row_top = jnp.where(mine, highest, row_top)
    owned = (owners >= 0.0) & head_lane
    scale = jnp.where(owned, jnp.exp(jnp.where(owned, all_top - row_top, 0.0)), 0.0)
    scaled_total = scale * all_total
    row_total = jnp.ones((NPP, LANES), F32)
    for r in range(R):
        mine = owners == float(r)
        summed = jnp.sum(jnp.where(mine, scaled_total, 0.0), axis=0, keepdims=True)
        row_total = jnp.where(mine, summed, row_total)
    share = jnp.where(owned, scale / jnp.where(owned, row_total, 1.0), 0.0).astype(BF16)

    for c in range(2):
        for src in ep_peers:
            remote(
                a_all.at[c, src], a_all.at[c, src], a_ss.at[c, 0], a_rs.at[c, src], (g, src)
            ).wait_recv()
        for s in range(n_ep):
            arrived = a_all[c, s].astype(F32)
            first = s * PD + c * part_pages
            for i, (low, high) in enumerate(QUARTERS):
                wv_ref[first:first + part_pages, low:high] = (
                    arrived[i * part_pages:(i + 1) * part_pages, 0:high - low]
                )
    attn = []
    for h in range(2):
        columns = slice(h * half, (h + 1) * half)
        terms = (dot(share, e_ref[:, columns]) * wv_ref[:, columns]).astype(BF16)
        attn.append(dot(o_ref[...], terms).astype(BF16))
    stream = [rs_ref[:, h * half:(h + 1) * half] + attn[h].astype(F32) for h in range(2)]
    square = sum(jnp.sum(s * s, axis=1, keepdims=True) for s in stream) * (1.0 / D)
    gain = gain_ref[...].astype(F32).reshape(1, D)
    inverse = lax.rsqrt(square + NORM_EPS)
    normed = [
        (stream[h] * inverse * gain[:, h * half:(h + 1) * half]).astype(BF16)
        for h in range(2)
    ]
    x_all[my_place] = jnp.concatenate([dot(pick, n) for n in normed], axis=0).astype(BF16)

    def x_copy(place, k, device):
        return remote(x_all.at[place], x_all.at[place], x_ss.at[k], x_rs.at[place], device)

    x_sends = [
        x_copy(my_place, k, (2 * peer + side, e)) for k, peer in enumerate(pair_peers)
    ]
    x_sends.append(x_copy(my_place, pairs - 1, (mate, e)))
    for copy in x_sends:
        copy.start()
    own_pick = jnp.where(iota((req_dev, R), 1) == iota((req_dev, R), 0) + e * req_dev, 1.0, 0.0)
    own_attn = [dot(own_pick.astype(BF16), a) for a in attn]
    for k, peer in enumerate(pair_peers):
        x_copy(mine_first + peer, 0, (mate, e)).wait_recv()
        forward = x_copy(mine_first + peer, pairs + k, (mate, e))
        forward.start()
        x_sends.append(forward)
    for copy in w_copies:
        copy.wait()
    for peer in [pair] + pair_peers:
        x_copy(mate_first + peer, 0, (mate, e)).wait_recv()

    rows_in = x_all[...].astype(F32)
    x_lo = rows_in[:, :slots, :].reshape(n_grp * slots, half).astype(BF16)
    x_hi = rows_in[:, slots:, :].reshape(n_grp * slots, half).astype(BF16)
    last = ((1,), (1,))
    gate_part = dot(x_lo, wg[:, 0:half], last) + dot(x_hi, wg[:, half:D], last)
    up_part = dot(x_lo, wu[:, 0:half], last) + dot(x_hi, wu[:, half:D], last)
    inner = (gate_part / (1.0 + jnp.exp(-gate_part)) * up_part).astype(BF16)

    width = D // CHUNKS
    piece = width // 2
    y_sends = []

    def pair_copy(c):
        return remote(
            y_send.at[c, pl.ds(mate_first, pairs)], y_pair.at[c], p_ss.at[c], p_rs.at[c], (mate, e)
        )

    def pair_sum(c):
        pair_copy(c).wait_recv()
        both = y_send[c, pl.ds(mine_first, pairs)].astype(F32) + y_pair[c].astype(F32)
        y_sum[c] = both.astype(BF16)
        for k, peer in enumerate(pair_peers):
            copy = remote(
                y_sum.at[c, peer], y_recv.at[c, pair], y_ss.at[c, k], y_rs.at[c, pair],
                (2 * peer + side, e),
            )
            copy.start()
            y_sends.append(copy)

    for c in range(CHUNKS):
        y_part = dot(inner, wd[:, c * width:(c + 1) * width])
        for h in range(2):
            y_send[c, :, h * slots:(h + 1) * slots, :] = (
                y_part[:, h * piece:(h + 1) * piece].reshape(n_grp, slots, piece).astype(BF16)
            )
        copy = pair_copy(c)
        copy.start()
        y_sends.append(copy)
        if c:
            pair_sum(c - 1)
    pair_sum(CHUNKS - 1)

    z_sends = []
    for c in range(CHUNKS):
        summed = y_sum[c, pair].astype(F32)
        for src in pair_peers:
            remote(
                y_sum.at[c, src], y_recv.at[c, src], y_ss.at[c, 0], y_rs.at[c, src],
                (2 * src + side, e),
            ).wait_recv()
            summed = summed + y_recv[c, src].astype(F32)
        summed = summed.astype(BF16).astype(F32)
        for s in range(n_ep):
            z_send[c, s, 0:cap, :] = summed[s * cap:(s + 1) * cap, :]
            z_send[c, s, cap:2 * cap, :] = summed[slots + s * cap:slots + (s + 1) * cap, :]
        sends = [
            remote(z_send.at[c, peer], z_recv.at[c, e], z_ss.at[c, k], z_rs.at[c, e], (g, peer))
            for k, peer in enumerate(ep_peers)
        ]
        for copy in sends:
            copy.start()
        z_recv[c, e] = z_send[c, e]
        z_sends += sends
    own_both = jnp.concatenate(own_attn, axis=1)
    for c in range(CHUNKS):
        for src in ep_peers:
            remote(
                z_send.at[c, src], z_recv.at[c, src], z_ss.at[c, 0], z_rs.at[c, src], (g, src)
            ).wait_recv()
        for h in range(2):
            start = c * width + h * piece
            update = own_both[:, start:start + piece]
            for s in range(n_ep):
                for i in range(cap):
                    slot = s * cap + i
                    row = h * cap + i
                    update = update + blend[:, slot:slot + 1] * z_recv[c, s, row:row + 1, :]
            out_ref[:, start:start + piece] = update.astype(BF16)

    for copy in r_sends + exchange + b_sends + x_sends + y_sends + z_sends:
        copy.wait_send()


def on_device(
    n_grp, n_ep,
    queries, residual, gain, key_pages, value_pages, page_table, lengths, split_flag,
    routes, gates, w_gate, w_up, w_down,
):
    req_dev, D = residual.shape
    R = queries.shape[0]
    PD = key_pages.shape[0]
    F = w_gate.shape[2]
    half = D // 2
    cap = max(2, (TOP * req_dev + n_ep - 1) // n_ep)
    slots = n_ep * cap
    n_pages = n_ep * PD
    NPP = -(-(n_pages + n_ep) // 16) * 16
    vmem = pl.BlockSpec(memory_space=pltpu.VMEM)
    smem = pl.BlockSpec(memory_space=pltpu.SMEM)
    hbm = pl.BlockSpec(memory_space=pl.ANY)
    dma = pltpu.SemaphoreType.DMA
    scratch = [
        pltpu.VMEM((PD, PAGE, D), BF16),
        pltpu.VMEM((PD, PAGE, D), BF16),
        pltpu.VMEM((F, D), BF16),
        pltpu.VMEM((F, D), BF16),
        pltpu.VMEM((F, D), BF16),
        pltpu.VMEM((LANES, D), BF16),
        pltpu.VMEM((PD, D), F32),
        pltpu.VMEM((PD, LANES), F32),
        pltpu.VMEM((LANES, LANES), F32),
        pltpu.VMEM((PD, D), F32),
        pltpu.VMEM((NPP, LANES), F32),
        pltpu.VMEM((R, NPP), BF16),
        pltpu.VMEM((NPP, D), F32),
        pltpu.VMEM((2 * PD, PART_COLS), F32),
        pltpu.VMEM((R, D), F32),
        pltpu.VMEM((R, LANES), F32),
        pltpu.VMEM((n_ep, 2 * req_dev, half + LANES), F32),
        pltpu.VMEM((n_ep, PD, LANES), F32),
        pltpu.VMEM((2, n_ep, 2 * PD, PART_COLS), BF16),
        pltpu.VMEM((8, B_COLS), F32),
        pltpu.VMEM((n_ep, 8, B_COLS), F32),
        pltpu.VMEM((n_grp, 2 * slots, half), BF16),
        pltpu.VMEM((CHUNKS, n_grp, 2 * slots, half // CHUNKS), BF16),
        pltpu.VMEM((CHUNKS, n_grp // 2, 2 * slots, half // CHUNKS), BF16),
        pltpu.VMEM((CHUNKS, n_grp // 2, 2 * slots, half // CHUNKS), BF16),
        pltpu.VMEM((CHUNKS, n_grp // 2, 2 * slots, half // CHUNKS), BF16),
        pltpu.VMEM((CHUNKS, n_ep, 2 * cap, half // CHUNKS), F32),
        pltpu.VMEM((CHUNKS, n_ep, 2 * cap, half // CHUNKS), F32),
        dma((2, PD)),
        dma((3,)),
    ]
    for shape in (
        (n_ep,), (n_ep,), (2, n_ep), (n_ep,), (n_grp,), (CHUNKS,), (CHUNKS, n_grp // 2),
        (CHUNKS, n_ep),
    ):
        scratch += [dma(shape), dma(shape)]
    return pl.pallas_call(
        functools.partial(fused, (n_grp, n_ep, cap)),
        out_shape=jax.ShapeDtypeStruct((req_dev, D), BF16),
        in_specs=[vmem] * 6 + [smem] * 2 + [hbm] * 5,
        out_specs=vmem,
        scratch_shapes=scratch,
        compiler_params=pltpu.CompilerParams(
            collective_id=0, has_side_effects=True, vmem_limit_bytes=56 * 1024 * 1024
        ),
    )(
        queries, residual, gain, page_table, routes.T, gates.T,
        lengths, split_flag,
        key_pages, value_pages, jnp.swapaxes(w_gate, 1, 2), jnp.swapaxes(w_up, 1, 2), w_down,
    )


def solution(mesh):
    in_specs = (
        P("grp", None),
        P(("grp", "ep"), None),
        P(),
        P(("grp", "ep"), None, None),
        P(("grp", "ep"), None, None),
        P("grp", None),
        P("grp"),
        P("grp"),
        P(("grp", "ep"), None),
        P(("grp", "ep"), None),
        P("ep", None, "grp"),
        P("ep", None, "grp"),
        P("ep", "grp", None),
    )
    return jax.shard_map(
        functools.partial(on_device, mesh.shape["grp"], mesh.shape["ep"]),
        mesh=mesh, in_specs=in_specs, out_specs=P(("grp", "ep"), None), check_vma=False,
    )
```

```python
import functools

import jax
import jax.numpy as jnp
from jax import lax
from jax.experimental import pallas as pl
from jax.experimental.pallas import tpu as pltpu
from jax.sharding import PartitionSpec as P

HEAD_DIM = 64
PAGE = 128
LANES = 128
NEG_FILL = -1e30
NEG_FLOOR = -1e29
NORM_EPS = 1e-06
TOP = 2
B_COLS = 384
CHUNKS = 3
OCTET = 8
V_COLS = 256
QUARTERS = ((0, 640), (640, 1280), (1280, 1792), (1792, 2304))
PART_COLS = 640

F32 = jnp.float32
BF16 = jnp.bfloat16


def iota(shape, axis):
    return lax.broadcasted_iota(jnp.int32, shape, axis)


def dot(a, b, contract=((1,), (0,))):
    return lax.dot_general(a, b, (contract, ((), ())), preferred_element_type=F32)


def fused(
    sizes,
    q_ref, res_ref, gain_ref, pt_ref, routes_ref, gates_ref,
    len_ref, split_ref,
    key_hbm, value_hbm, wg_hbm, wu_hbm, wd_hbm,
    out_ref,
    kbuf, vbuf, wg, wu, wd,
    e_ref, qp_ref, lim_ref, st_ref, w_ref, own_ref, o_ref,
    wv_ref, af_ref, rs_ref, rt_ref,
    r_all, st_all, a_all, b_send, b_recv, x_all, y_send, y_pair, y_sum, y_recv, z_send, z_recv,
    kv_sem, w_sem,
    r_ss, r_rs, st_ss, st_rs, a_ss, a_rs, b_ss, b_rs, x_ss, x_rs, p_ss, p_rs, y_ss, y_rs, z_ss, z_rs,
):
    n_grp, n_ep, cap = sizes
    req_dev, D = res_ref.shape
    R = q_ref.shape[0]
    J = pt_ref.shape[1]
    PD = key_hbm.shape[0]
    half = D // 2
    heads = D // HEAD_DIM
    HP = -(-heads // OCTET) * OCTET
    slots = n_ep * cap
    NPP = own_ref.shape[0]
    n_pages = n_ep * PD

    g = lax.axis_index("grp")
    e = lax.axis_index("ep")
    mate = g + 1 - 2 * lax.rem(g, 2)

    ep_peers = [lax.rem(e + k, n_ep) for k in range(1, n_ep)]
    pairs = n_grp // 2
    side = lax.rem(g, 2)
    pair = lax.div(g, 2)
    pair_peers = [lax.rem(pair + k, pairs) for k in range(1, pairs)]
    mine_first, mate_first = side * pairs, (1 - side) * pairs
    my_place = mine_first + pair

    barrier = pltpu.get_barrier_semaphore()
    for peer in ep_peers:
        pl.semaphore_signal(barrier, inc=1, device_id=(g, peer), device_id_type=pl.DeviceIdType.MESH)
    for peer in pair_peers:
        pl.semaphore_signal(
            barrier, inc=1, device_id=(2 * peer + side, e), device_id_type=pl.DeviceIdType.MESH
        )
    for peer in [e] + ep_peers:
        pl.semaphore_signal(barrier, inc=1, device_id=(mate, peer), device_id_type=pl.DeviceIdType.MESH)

    def kv_copy(p, which):
        source, held = ((key_hbm, kbuf), (value_hbm, vbuf))[which]
        return pltpu.make_async_copy(source.at[p], held.at[p], kv_sem.at[which, p])

    part_pages = PD // 2
    for c in range(2):
        for which in range(2):
            for p in range(c * part_pages, (c + 1) * part_pages):
                kv_copy(p, which).start()
    w_copies = [
        pltpu.make_async_copy(wg_hbm.at[0], wg, w_sem.at[0]),
        pltpu.make_async_copy(wu_hbm.at[0], wu, w_sem.at[1]),
        pltpu.make_async_copy(wd_hbm.at[0], wd, w_sem.at[2]),
    ]

    def remote(src, dst, ss, rs, device):
        return pltpu.make_async_remote_copy(
            src_ref=src, dst_ref=dst, send_sem=ss, recv_sem=rs,
            device_id=device, device_id_type=pl.DeviceIdType.MESH,
        )

    res = res_ref[...].astype(F32)
    r_all[e, 0:req_dev, 0:half] = res[:, :half]
    r_all[e, req_dev:2 * req_dev, 0:half] = res[:, half:]
    route_lane = iota((2 * req_dev, LANES), 1)
    eye = iota((req_dev, req_dev), 0) == iota((req_dev, req_dev), 1)

    def column(row):
        return jnp.sum(jnp.where(eye, row, 0.0), axis=1, keepdims=True)

    routes_t = routes_ref[...].astype(F32)
    gates_t = gates_ref[...].astype(F32)
    routes = [column(routes_t[k:k + 1, :]) for k in range(TOP)]
    gates = [column(gates_t[k:k + 1, :]) for k in range(TOP)]
    r_all[e, :, half:half + LANES] = jnp.zeros((2 * req_dev, LANES), F32)
    r_all[e, 0:req_dev, half:half + LANES] = jnp.where(
        route_lane[:req_dev] == 0, routes[0],
        jnp.where(route_lane[:req_dev] == 1, routes[1], 0.0),
    )
    first_col = iota((LANES, D), 0) * HEAD_DIM
    col = iota((LANES, D), 1)
    in_head = (col >= first_col) & (col < first_col + HEAD_DIM)
    e_ref[...] = jnp.where(in_head, 1.0, 0.0).astype(BF16)
    st_ref[...] = jnp.zeros_like(st_ref)
    wv_ref[n_pages:, :] = jnp.zeros((NPP - n_pages, D), F32)

    split_row = 0
    for r in range(R):
        split_row = split_row + jnp.where(split_ref[r] == 1, r, 0)

    page_id = iota((NPP, J), 0)
    j_start = iota((1, J), 1) * PAGE
    local_id = iota((PD, J), 0) + e * PD
    owner = jnp.full((NPP, J), -1.0, F32)
    own_local = jnp.full((PD, J), -1.0, F32)
    limit = jnp.zeros((PD, J), F32)
    length_col = jnp.zeros((R, 1), jnp.int32)
    split_col = jnp.zeros((R, 1), jnp.int32)
    row_col = iota((R, 1), 0)
    for r in range(R):
        length = len_ref[r]
        entries = jnp.where(j_start < length, pt_ref[r:r + 1, :], -1)
        owner = jnp.where(page_id == entries, float(r), owner)
        hit = local_id == entries
        own_local = jnp.where(hit, float(r), own_local)
        limit = jnp.where(hit, jnp.minimum(length - j_start, PAGE).astype(F32), limit)
        length_col = jnp.where(row_col == r, length, length_col)
        split_col = jnp.where(row_col == r, split_ref[r], split_col)
    owner = jnp.max(owner, axis=1, keepdims=True)
    page_col = iota((NPP, LANES), 0)
    mate_pages = (page_col >= n_pages) & (page_col < n_pages + n_ep)
    own_ref[...] = jnp.where(
        mate_pages, split_row.astype(F32), jnp.broadcast_to(owner, (NPP, LANES))
    )
    own_local = jnp.max(own_local, axis=1, keepdims=True)
    limit = jnp.sum(limit, axis=1, keepdims=True)
    lim_ref[...] = jnp.broadcast_to(limit, (PD, LANES))
    split_local = jnp.broadcast_to(own_local, (PD, LANES)) == split_row.astype(F32)

    page_lane = iota((R, NPP), 1)
    o_rows = jnp.where(
        (page_lane >= n_pages) & (page_lane < n_pages + n_ep) & (split_col == 1), 1.0, 0.0
    )
    for j in range(J):
        entry = jnp.where(length_col > j * PAGE, pt_ref[:, j:j + 1], -1)
        o_rows = jnp.where(page_lane == entry, 1.0, o_rows)
    o_ref[...] = o_rows.astype(BF16)

    queries = q_ref[...].astype(F32)
    page_q = jnp.zeros((PD, D), F32)
    for r in range(R):
        page_q = jnp.where(own_local == float(r), queries[r:r + 1, :], page_q)
    qp_ref[...] = page_q

    token = iota((PAGE, HP), 0).astype(F32)
    af_ref[...] = jnp.zeros_like(af_ref)

    def part(c):
        first = c * part_pages
        for p in range(first, first + part_pages):
            kv_copy(p, 0).wait()
        scores = []
        for p in range(first, first + part_pages):
            q_heads = jnp.broadcast_to(qp_ref[p:p + 1, :].astype(BF16), (HP, D)) * e_ref[0:HP, :]
            page_scores = dot(kbuf[p], q_heads, ((1,), (1,))) * HEAD_DIM ** (-0.5)
            scores.append(jnp.where(token < lim_ref[p:p + 1, 0:1], page_scores, NEG_FILL))
        weights = []
        for i in range(part_pages):
            p = first + i
            top = jnp.maximum(jnp.max(scores[i], axis=0, keepdims=True), NEG_FLOOR)
            terms = jnp.exp(scores[i] - top)
            st_ref[p:p + 1, 0:HP] = top
            st_ref[p:p + 1, 64:64 + HP] = jnp.sum(terms, axis=0, keepdims=True)
            weights.append(terms.astype(BF16))
        weights = jnp.concatenate(weights, axis=0)
        for p in range(first, first + part_pages):
            kv_copy(p, 1).wait()
        if c:
            for copy in w_copies:
                copy.start()
        for low in range(0, D, V_COLS):
            columns = slice(low, low + V_COLS)
            spread = dot(weights, e_ref[0:HP, columns]).reshape(part_pages, PAGE, V_COLS)
            w_ref[first:first + part_pages, columns] = jnp.sum(
                spread * vbuf[first:first + part_pages, :, columns].astype(F32), axis=1
            )
        for i, (low, high) in enumerate(QUARTERS):
            af_ref[i * part_pages:(i + 1) * part_pages, 0:high - low] = (
                w_ref[first:first + part_pages, low:high]
            )
        a_all[c, e] = af_ref[...].astype(BF16)

    exchange = []

    def send_part(c):
        for k, peer in enumerate(ep_peers):
            copy = remote(
                a_all.at[c, e], a_all.at[c, e], a_ss.at[c, k], a_rs.at[c, e], (g, peer)
            )
            copy.start()
            exchange.append(copy)

    part(0)
    pl.semaphore_wait(barrier, 2 * n_ep - 1 + pairs - 1)
    r_sends = [
        remote(r_all.at[e], r_all.at[e], r_ss.at[k], r_rs.at[e], (g, peer))
        for k, peer in enumerate(ep_peers)
    ]
    for copy in r_sends:
        copy.start()
    send_part(0)
    part(1)
    send_part(1)

    head_lane = iota((1, LANES), 1) < heads

    stats = st_ref[...]
    st_all[e] = stats
    for k, peer in enumerate(ep_peers):
        copy = remote(st_all.at[e], st_all.at[e], st_ss.at[k], st_rs.at[e], (g, peer))
        copy.start()
        exchange.append(copy)

    totals = pltpu.roll(stats, 64, 1)
    split_top = jnp.max(jnp.where(split_local, stats, NEG_FILL), axis=0, keepdims=True)
    factor = jnp.where(split_local & head_lane, jnp.exp(stats - split_top), 0.0)
    split_total = jnp.sum(factor * totals, axis=0, keepdims=True)
    split_part = jnp.sum(dot(factor.astype(BF16), e_ref[...]) * w_ref[...], axis=0, keepdims=True)
    b_send[...] = jnp.zeros_like(b_send)
    b_rows = D // B_COLS
    for i in range(b_rows):
        b_send[i:i + 1, :] = split_part[:, i * B_COLS:(i + 1) * B_COLS]
    b_send[b_rows:b_rows + 1, 0:LANES] = split_top
    b_send[b_rows:b_rows + 1, LANES:2 * LANES] = split_total
    b_targets = [e] + ep_peers
    b_sends = [
        remote(b_send, b_recv.at[e], b_ss.at[k], b_rs.at[e], (mate, peer))
        for k, peer in enumerate(b_targets)
    ]
    for copy in b_sends:
        copy.start()

    for src in ep_peers:
        remote(r_all.at[src], r_all.at[src], r_ss.at[0], r_rs.at[src], (g, src)).wait_recv()
    for s in range(n_ep):
        rows = slice(s * req_dev, (s + 1) * req_dev)
        rs_ref[rows, 0:half] = r_all[s, 0:req_dev, 0:half]
        rs_ref[rows, half:D] = r_all[s, req_dev:2 * req_dev, 0:half]
        rt_ref[rows, :] = r_all[s, 0:req_dev, half:half + LANES]

    expert = e.astype(F32)
    chosen = rt_ref[...]
    has_col = jnp.where((chosen[:, 0:1] == expert) | (chosen[:, 1:2] == expert), 1.0, 0.0)
    r_sub = iota((R, R), 0)
    r_lane = iota((R, R), 1)
    has_row = jnp.sum(jnp.where(r_sub == r_lane, has_col, 0.0), axis=0, keepdims=True)
    earlier = (r_sub < r_lane) & (r_sub // req_dev == r_lane // req_dev)
    rank_row = jnp.sum(jnp.where(earlier, has_col, 0.0), axis=0, keepdims=True)
    slot_sub = iota((slots, R), 0)
    slot_row = iota((slots, R), 1)
    pick = jnp.where(
        (slot_sub // cap == slot_row // req_dev)
        & (has_row > 0.5)
        & (rank_row == (slot_sub % cap).astype(F32)),
        1.0, 0.0,
    ).astype(BF16)

    slot_lane = iota((req_dev, LANES), 1)
    slot_expert = (slot_lane // cap).astype(F32)
    first_hit = slot_expert == routes[0]
    second_hit = slot_expert == routes[1]
    hits = jnp.where(first_hit | second_hit, 1.0, 0.0)
    row_sub = iota((req_dev, LANES), 0)
    rank = jnp.zeros((req_dev, LANES), F32)
    for i in range(req_dev - 1):
        rank = rank + jnp.where(row_sub > i, hits[i:i + 1, :], 0.0)
    blend = jnp.where(first_hit, gates[0], 0.0) + jnp.where(second_hit, gates[1], 0.0)
    blend = jnp.where(rank == (slot_lane % cap).astype(F32), blend, 0.0)

    for src in ep_peers:
        remote(st_all.at[src], st_all.at[src], st_ss.at[0], st_rs.at[src], (g, src)).wait_recv()
    for src in b_targets:
        remote(b_send, b_recv.at[src], b_ss.at[0], b_rs.at[src], (mate, src)).wait_recv()
    extra = NPP - n_pages
    extra_sub = iota((extra, LANES), 0)
    extra_top = jnp.full((extra, LANES), NEG_FILL, F32)
    extra_total = jnp.zeros((extra, LANES), F32)
    for s in range(n_ep):
        extra_top = jnp.where(extra_sub == s, b_recv[s, b_rows:b_rows + 1, 0:LANES], extra_top)
        extra_total = jnp.where(
            extra_sub == s, b_recv[s, b_rows:b_rows + 1, LANES:2 * LANES], extra_total
        )
        for i in range(b_rows):
            row = n_pages + s
            wv_ref[row:row + 1, i * B_COLS:(i + 1) * B_COLS] = b_recv[s, i:i + 1, :]
    all_stats = st_all[...].reshape(n_pages, LANES)
    all_top = jnp.concatenate([all_stats, extra_top], axis=0)
    all_total = jnp.concatenate([pltpu.roll(all_stats, 64, 1), extra_total], axis=0)
    owners = own_ref[...]
    row_top = jnp.zeros((NPP, LANES), F32)
    for r in range(R):
        mine = owners == float(r)
        highest = jnp.max(jnp.where(mine, all_top, NEG_FILL), axis=0, keepdims=True)
        row_top = jnp.where(mine, highest, row_top)
    owned = (owners >= 0.0) & head_lane
    scale = jnp.where(owned, jnp.exp(jnp.where(owned, all_top - row_top, 0.0)), 0.0)
    scaled_total = scale * all_total
    row_total = jnp.ones((NPP, LANES), F32)
    for r in range(R):
        mine = owners == float(r)
        summed = jnp.sum(jnp.where(mine, scaled_total, 0.0), axis=0, keepdims=True)
        row_total = jnp.where(mine, summed, row_total)
    share = jnp.where(owned, scale / jnp.where(owned, row_total, 1.0), 0.0).astype(BF16)

    for c in range(2):
        for src in ep_peers:
            remote(
                a_all.at[c, src], a_all.at[c, src], a_ss.at[c, 0], a_rs.at[c, src], (g, src)
            ).wait_recv()
        for s in range(n_ep):
            arrived = a_all[c, s].astype(F32)
            first = s * PD + c * part_pages
            for i, (low, high) in enumerate(QUARTERS):
                wv_ref[first:first + part_pages, low:high] = (
                    arrived[i * part_pages:(i + 1) * part_pages, 0:high - low]
                )
    attn = []
    for h in range(2):
        columns = slice(h * half, (h + 1) * half)
        terms = (dot(share, e_ref[:, columns]) * wv_ref[:, columns]).astype(BF16)
        attn.append(dot(o_ref[...], terms).astype(BF16))
    stream = [rs_ref[:, h * half:(h + 1) * half] + attn[h].astype(F32) for h in range(2)]
    square = sum(jnp.sum(s * s, axis=1, keepdims=True) for s in stream) * (1.0 / D)
    gain = gain_ref[...].astype(F32).reshape(1, D)
    inverse = lax.rsqrt(square + NORM_EPS)
    normed = [
        (stream[h] * inverse * gain[:, h * half:(h + 1) * half]).astype(BF16)
        for h in range(2)
    ]
    x_all[my_place] = jnp.concatenate([dot(pick, n) for n in normed], axis=0).astype(BF16)

    def x_copy(place, k, device):
        return remote(x_all.at[place], x_all.at[place], x_ss.at[k], x_rs.at[place], device)

    x_sends = [
        x_copy(my_place, k, (2 * peer + side, e)) for k, peer in enumerate(pair_peers)
    ]
    x_sends.append(x_copy(my_place, pairs - 1, (mate, e)))
    for copy in x_sends:
        copy.start()
    own_pick = jnp.where(iota((req_dev, R), 1) == iota((req_dev, R), 0) + e * req_dev, 1.0, 0.0)
    own_attn = [dot(own_pick.astype(BF16), a) for a in attn]
    for k, peer in enumerate(pair_peers):
        x_copy(mine_first + peer, 0, (mate, e)).wait_recv()
        forward = x_copy(mine_first + peer, pairs + k, (mate, e))
        forward.start()
        x_sends.append(forward)
    for copy in w_copies:
        copy.wait()
    for peer in [pair] + pair_peers:
        x_copy(mate_first + peer, 0, (mate, e)).wait_recv()

    rows_in = x_all[...].astype(F32)
    x_lo = rows_in[:, :slots, :].reshape(n_grp * slots, half).astype(BF16)
    x_hi = rows_in[:, slots:, :].reshape(n_grp * slots, half).astype(BF16)
    x_rows = jnp.concatenate([x_lo, x_hi], axis=1)
    gate_part = dot(wg[...], x_rows, ((1,), (1,)))
    up_part = dot(wu[...], x_rows, ((1,), (1,)))
    inner = gate_part / (1.0 + jnp.exp(-gate_part)) * up_part
    inner = jnp.transpose(inner).astype(BF16)

    width = D // CHUNKS
    piece = width // 2
    y_sends = []

    def pair_copy(c):
        return remote(
            y_send.at[c, pl.ds(mate_first, pairs)], y_pair.at[c], p_ss.at[c], p_rs.at[c], (mate, e)
        )

    def pair_sum(c):
        pair_copy(c).wait_recv()
        both = y_send[c, pl.ds(mine_first, pairs)].astype(F32) + y_pair[c].astype(F32)
        y_sum[c] = both.astype(BF16)
        for k, peer in enumerate(pair_peers):
            copy = remote(
                y_sum.at[c, peer], y_recv.at[c, pair], y_ss.at[c, k], y_rs.at[c, pair],
                (2 * peer + side, e),
            )
            copy.start()
            y_sends.append(copy)

    for c in range(CHUNKS):
        y_part = dot(inner, wd[:, c * width:(c + 1) * width])
        for h in range(2):
            y_send[c, :, h * slots:(h + 1) * slots, :] = (
                y_part[:, h * piece:(h + 1) * piece].reshape(n_grp, slots, piece).astype(BF16)
            )
        copy = pair_copy(c)
        copy.start()
        y_sends.append(copy)
        if c:
            pair_sum(c - 1)
    pair_sum(CHUNKS - 1)

    z_sends = []
    for c in range(CHUNKS):
        summed = y_sum[c, pair].astype(F32)
        for src in pair_peers:
            remote(
                y_sum.at[c, src], y_recv.at[c, src], y_ss.at[c, 0], y_rs.at[c, src],
                (2 * src + side, e),
            ).wait_recv()
            summed = summed + y_recv[c, src].astype(F32)
        summed = summed.astype(BF16).astype(F32)
        for s in range(n_ep):
            z_send[c, s, 0:cap, :] = summed[s * cap:(s + 1) * cap, :]
            z_send[c, s, cap:2 * cap, :] = summed[slots + s * cap:slots + (s + 1) * cap, :]
        sends = [
            remote(z_send.at[c, peer], z_recv.at[c, e], z_ss.at[c, k], z_rs.at[c, e], (g, peer))
            for k, peer in enumerate(ep_peers)
        ]
        for copy in sends:
            copy.start()
        z_recv[c, e] = z_send[c, e]
        z_sends += sends
    own_both = jnp.concatenate(own_attn, axis=1)
    for c in range(CHUNKS):
        for src in ep_peers:
            remote(
                z_send.at[c, src], z_recv.at[c, src], z_ss.at[c, 0], z_rs.at[c, src], (g, src)
            ).wait_recv()
        for h in range(2):
            start = c * width + h * piece
            update = own_both[:, start:start + piece]
            for s in range(n_ep):
                for i in range(cap):
                    slot = s * cap + i
                    row = h * cap + i
                    update = update + blend[:, slot:slot + 1] * z_recv[c, s, row:row + 1, :]
            out_ref[:, start:start + piece] = update.astype(BF16)

    for copy in r_sends + exchange + b_sends + x_sends + y_sends + z_sends:
        copy.wait_send()


def on_device(
    n_grp, n_ep,
    queries, residual, gain, key_pages, value_pages, page_table, lengths, split_flag,
    routes, gates, w_gate, w_up, w_down,
):
    req_dev, D = residual.shape
    R = queries.shape[0]
    PD = key_pages.shape[0]
    F = w_gate.shape[2]
    half = D // 2
    cap = max(2, (TOP * req_dev + n_ep - 1) // n_ep)
    slots = n_ep * cap
    n_pages = n_ep * PD
    NPP = -(-(n_pages + n_ep) // 16) * 16
    vmem = pl.BlockSpec(memory_space=pltpu.VMEM)
    smem = pl.BlockSpec(memory_space=pltpu.SMEM)
    hbm = pl.BlockSpec(memory_space=pl.ANY)
    dma = pltpu.SemaphoreType.DMA
    scratch = [
        pltpu.VMEM((PD, PAGE, D), BF16),
        pltpu.VMEM((PD, PAGE, D), BF16),
        pltpu.VMEM((F, D), BF16),
        pltpu.VMEM((F, D), BF16),
        pltpu.VMEM((F, D), BF16),
        pltpu.VMEM((LANES, D), BF16),
        pltpu.VMEM((PD, D), F32),
        pltpu.VMEM((PD, LANES), F32),
        pltpu.VMEM((PD, LANES), F32),
        pltpu.VMEM((PD, D), F32),
        pltpu.VMEM((NPP, LANES), F32),
        pltpu.VMEM((R, NPP), BF16),
        pltpu.VMEM((NPP, D), F32),
        pltpu.VMEM((2 * PD, PART_COLS), F32),
        pltpu.VMEM((R, D), F32),
        pltpu.VMEM((R, LANES), F32),
        pltpu.VMEM((n_ep, 2 * req_dev, half + LANES), F32),
        pltpu.VMEM((n_ep, PD, LANES), F32),
        pltpu.VMEM((2, n_ep, 2 * PD, PART_COLS), BF16),
        pltpu.VMEM((8, B_COLS), F32),
        pltpu.VMEM((n_ep, 8, B_COLS), F32),
        pltpu.VMEM((n_grp, 2 * slots, half), BF16),
        pltpu.VMEM((CHUNKS, n_grp, 2 * slots, half // CHUNKS), BF16),
        pltpu.VMEM((CHUNKS, n_grp // 2, 2 * slots, half // CHUNKS), BF16),
        pltpu.VMEM((CHUNKS, n_grp // 2, 2 * slots, half // CHUNKS), BF16),
        pltpu.VMEM((CHUNKS, n_grp // 2, 2 * slots, half // CHUNKS), BF16),
        pltpu.VMEM((CHUNKS, n_ep, 2 * cap, half // CHUNKS), F32),
        pltpu.VMEM((CHUNKS, n_ep, 2 * cap, half // CHUNKS), F32),
        dma((2, PD)),
        dma((3,)),
    ]
    for shape in (
        (n_ep,), (n_ep,), (2, n_ep), (n_ep,), (n_grp,), (CHUNKS,), (CHUNKS, n_grp // 2),
        (CHUNKS, n_ep),
    ):
        scratch += [dma(shape), dma(shape)]
    return pl.pallas_call(
        functools.partial(fused, (n_grp, n_ep, cap)),
        out_shape=jax.ShapeDtypeStruct((req_dev, D), BF16),
        in_specs=[vmem] * 6 + [smem] * 2 + [hbm] * 5,
        out_specs=vmem,
        scratch_shapes=scratch,
        compiler_params=pltpu.CompilerParams(
            collective_id=0, has_side_effects=True, vmem_limit_bytes=56 * 1024 * 1024
        ),
    )(
        queries, residual, gain, page_table, routes.T, gates.T,
        lengths, split_flag,
        key_pages, value_pages, jnp.swapaxes(w_gate, 1, 2), jnp.swapaxes(w_up, 1, 2), w_down,
    )


def solution(mesh):
    in_specs = (
        P("grp", None),
        P(("grp", "ep"), None),
        P(),
        P(("grp", "ep"), None, None),
        P(("grp", "ep"), None, None),
        P("grp", None),
        P("grp"),
        P("grp"),
        P(("grp", "ep"), None),
        P(("grp", "ep"), None),
        P("ep", None, "grp"),
        P("ep", None, "grp"),
        P("ep", "grp", None),
    )
    return jax.shard_map(
        functools.partial(on_device, mesh.shape["grp"], mesh.shape["ep"]),
        mesh=mesh, in_specs=in_specs, out_specs=P(("grp", "ep"), None), check_vma=False,
    )
```

```python
import functools

import jax
import jax.numpy as jnp
from jax import lax
from jax.experimental import pallas as pl
from jax.experimental.pallas import tpu as pltpu
from jax.sharding import PartitionSpec as P

HEAD_DIM = 64
PAGE = 128
LANES = 128
NEG_FILL = -1e30
NEG_FLOOR = -1e29
NORM_EPS = 1e-06
TOP = 2
B_COLS = 384
CHUNKS = 3
OCTET = 8
V_COLS = 256
QUARTERS = ((0, 640), (640, 1280), (1280, 1792), (1792, 2304))
PART_COLS = 640
ROUTE_PART = 2
ROUTE_COL = 512

F32 = jnp.float32
BF16 = jnp.bfloat16


def iota(shape, axis):
    return lax.broadcasted_iota(jnp.int32, shape, axis)


def dot(a, b, contract=((1,), (0,))):
    return lax.dot_general(a, b, (contract, ((), ())), preferred_element_type=F32)


def fused(
    sizes,
    q_ref, res_ref, gain_ref, pt_ref, routes_ref, gates_ref,
    len_ref, split_ref,
    key_hbm, value_hbm, wg_hbm, wu_hbm, wd_hbm,
    out_ref,
    kbuf, vbuf, wg, wu, wd,
    e_ref, qp_ref, lim_ref, st_ref, w_ref, own_ref, o_ref,
    wv_ref, af_ref, rs_ref, rt_ref,
    r_all, st_all, a_all, b_send, b_recv, x_all, y_send, y_pair, y_sum, y_recv, z_send, z_recv,
    kv_sem, w_sem,
    r_ss, r_rs, st_ss, st_rs, a_ss, a_rs, b_ss, b_rs, x_ss, x_rs, p_ss, p_rs, y_ss, y_rs, z_ss, z_rs,
):
    n_grp, n_ep, cap = sizes
    req_dev, D = res_ref.shape
    R = q_ref.shape[0]
    J = pt_ref.shape[1]
    PD = key_hbm.shape[0]
    half = D // 2
    heads = D // HEAD_DIM
    HP = -(-heads // OCTET) * OCTET
    slots = n_ep * cap
    NPP = own_ref.shape[0]
    n_pages = n_ep * PD

    g = lax.axis_index("grp")
    e = lax.axis_index("ep")
    mate = g + 1 - 2 * lax.rem(g, 2)

    ep_peers = [lax.rem(e + k, n_ep) for k in range(1, n_ep)]
    pairs = n_grp // 2
    side = lax.rem(g, 2)
    pair = lax.div(g, 2)
    pair_peers = [lax.rem(pair + k, pairs) for k in range(1, pairs)]
    mine_first, mate_first = side * pairs, (1 - side) * pairs
    my_place = mine_first + pair

    barrier = pltpu.get_barrier_semaphore()
    for peer in ep_peers:
        pl.semaphore_signal(barrier, inc=1, device_id=(g, peer), device_id_type=pl.DeviceIdType.MESH)
    for peer in pair_peers:
        pl.semaphore_signal(
            barrier, inc=1, device_id=(2 * peer + side, e), device_id_type=pl.DeviceIdType.MESH
        )
    for peer in [e] + ep_peers:
        pl.semaphore_signal(barrier, inc=1, device_id=(mate, peer), device_id_type=pl.DeviceIdType.MESH)

    def kv_copy(p, which):
        source, held = ((key_hbm, kbuf), (value_hbm, vbuf))[which]
        return pltpu.make_async_copy(source.at[p], held.at[p], kv_sem.at[which, p])

    part_pages = PD // 2
    for c in range(2):
        for which in range(2):
            for p in range(c * part_pages, (c + 1) * part_pages):
                kv_copy(p, which).start()
    w_copies = [
        pltpu.make_async_copy(wg_hbm.at[0], wg, w_sem.at[0]),
        pltpu.make_async_copy(wu_hbm.at[0], wu, w_sem.at[1]),
        pltpu.make_async_copy(wd_hbm.at[0], wd, w_sem.at[2]),
    ]

    def remote(src, dst, ss, rs, device):
        return pltpu.make_async_remote_copy(
            src_ref=src, dst_ref=dst, send_sem=ss, recv_sem=rs,
            device_id=device, device_id_type=pl.DeviceIdType.MESH,
        )

    eye = iota((req_dev, req_dev), 0) == iota((req_dev, req_dev), 1)

    def column(row):
        return jnp.sum(jnp.where(eye, row, 0.0), axis=1, keepdims=True)

    routes_t = routes_ref[...].astype(F32)
    gates_t = gates_ref[...].astype(F32)
    routes = [column(routes_t[k:k + 1, :]) for k in range(TOP)]
    gates = [column(gates_t[k:k + 1, :]) for k in range(TOP)]
    route_lane = iota((req_dev, LANES), 1)
    af_ref[...] = jnp.zeros_like(af_ref)
    res = res_ref[...].astype(F32)
    for i, (low, high) in enumerate(QUARTERS):
        af_ref[i * req_dev:(i + 1) * req_dev, 0:high - low] = res[:, low:high]
    af_ref[ROUTE_PART * req_dev:(ROUTE_PART + 1) * req_dev, ROUTE_COL:PART_COLS] = jnp.where(
        route_lane == 0, routes[0], jnp.where(route_lane == 1, routes[1], 0.0)
    )
    r_all[e] = af_ref[...].astype(BF16)

    first_col = iota((LANES, D), 0) * HEAD_DIM
    col = iota((LANES, D), 1)
    in_head = (col >= first_col) & (col < first_col + HEAD_DIM)
    e_ref[...] = jnp.where(in_head, 1.0, 0.0).astype(BF16)
    st_ref[...] = jnp.zeros_like(st_ref)
    wv_ref[n_pages:, :] = jnp.zeros((NPP - n_pages, D), F32)

    split_row = 0
    for r in range(R):
        split_row = split_row + jnp.where(split_ref[r] == 1, r, 0)

    page_id = iota((NPP, J), 0)
    j_start = iota((1, J), 1) * PAGE
    local_id = iota((PD, J), 0) + e * PD
    owner = jnp.full((NPP, J), -1.0, F32)
    own_local = jnp.full((PD, J), -1.0, F32)
    limit = jnp.zeros((PD, J), F32)
    length_col = jnp.zeros((R, 1), jnp.int32)
    split_col = jnp.zeros((R, 1), jnp.int32)
    row_col = iota((R, 1), 0)
    for r in range(R):
        length = len_ref[r]
        entries = jnp.where(j_start < length, pt_ref[r:r + 1, :], -1)
        owner = jnp.where(page_id == entries, float(r), owner)
        hit = local_id == entries
        own_local = jnp.where(hit, float(r), own_local)
        limit = jnp.where(hit, jnp.minimum(length - j_start, PAGE).astype(F32), limit)
        length_col = jnp.where(row_col == r, length, length_col)
        split_col = jnp.where(row_col == r, split_ref[r], split_col)
    owner = jnp.max(owner, axis=1, keepdims=True)
    page_col = iota((NPP, LANES), 0)
    mate_pages = (page_col >= n_pages) & (page_col < n_pages + n_ep)
    own_ref[...] = jnp.where(
        mate_pages, split_row.astype(F32), jnp.broadcast_to(owner, (NPP, LANES))
    )
    own_local = jnp.max(own_local, axis=1, keepdims=True)
    limit = jnp.sum(limit, axis=1, keepdims=True)
    lim_ref[...] = jnp.broadcast_to(limit, (PD, LANES))
    split_local = jnp.broadcast_to(own_local, (PD, LANES)) == split_row.astype(F32)

    page_lane = iota((R, NPP), 1)
    o_rows = jnp.where(
        (page_lane >= n_pages) & (page_lane < n_pages + n_ep) & (split_col == 1), 1.0, 0.0
    )
    for j in range(J):
        entry = jnp.where(length_col > j * PAGE, pt_ref[:, j:j + 1], -1)
        o_rows = jnp.where(page_lane == entry, 1.0, o_rows)
    o_ref[...] = o_rows.astype(BF16)

    queries = q_ref[...].astype(F32)
    page_q = jnp.zeros((PD, D), F32)
    for r in range(R):
        page_q = jnp.where(own_local == float(r), queries[r:r + 1, :], page_q)
    qp_ref[...] = page_q

    token = iota((PAGE, HP), 0).astype(F32)

    def part(c):
        first = c * part_pages
        for p in range(first, first + part_pages):
            kv_copy(p, 0).wait()
        scores = []
        for p in range(first, first + part_pages):
            q_heads = jnp.broadcast_to(qp_ref[p:p + 1, :].astype(BF16), (HP, D)) * e_ref[0:HP, :]
            page_scores = dot(kbuf[p], q_heads, ((1,), (1,))) * HEAD_DIM ** (-0.5)
            scores.append(jnp.where(token < lim_ref[p:p + 1, 0:1], page_scores, NEG_FILL))
        weights = []
        for i in range(part_pages):
            p = first + i
            top = jnp.maximum(jnp.max(scores[i], axis=0, keepdims=True), NEG_FLOOR)
            terms = jnp.exp(scores[i] - top)
            st_ref[p:p + 1, 0:HP] = top
            st_ref[p:p + 1, 64:64 + HP] = jnp.sum(terms, axis=0, keepdims=True)
            weights.append(terms.astype(BF16))
        weights = jnp.concatenate(weights, axis=0)
        for p in range(first, first + part_pages):
            kv_copy(p, 1).wait()
        if c:
            for copy in w_copies:
                copy.start()
        for low in range(0, D, V_COLS):
            columns = slice(low, low + V_COLS)
            spread = dot(weights, e_ref[0:HP, columns]).reshape(part_pages, PAGE, V_COLS)
            w_ref[first:first + part_pages, columns] = jnp.sum(
                spread * vbuf[first:first + part_pages, :, columns].astype(F32), axis=1
            )
        for i, (low, high) in enumerate(QUARTERS):
            af_ref[i * part_pages:(i + 1) * part_pages, 0:high - low] = (
                w_ref[first:first + part_pages, low:high]
            )
        a_all[c, e] = af_ref[...].astype(BF16)

    exchange = []

    def send_part(c):
        for k, peer in enumerate(ep_peers):
            copy = remote(
                a_all.at[c, e], a_all.at[c, e], a_ss.at[c, k], a_rs.at[c, e], (g, peer)
            )
            copy.start()
            exchange.append(copy)

    pl.semaphore_wait(barrier, 2 * n_ep - 1 + pairs - 1)
    r_sends = [
        remote(r_all.at[e], r_all.at[e], r_ss.at[k], r_rs.at[e], (g, peer))
        for k, peer in enumerate(ep_peers)
    ]
    for copy in r_sends:
        copy.start()
    part(0)
    send_part(0)
    part(1)
    send_part(1)

    head_lane = iota((1, LANES), 1) < heads

    stats = st_ref[...]
    st_all[e] = stats
    for k, peer in enumerate(ep_peers):
        copy = remote(st_all.at[e], st_all.at[e], st_ss.at[k], st_rs.at[e], (g, peer))
        copy.start()
        exchange.append(copy)

    totals = pltpu.roll(stats, 64, 1)
    split_top = jnp.max(jnp.where(split_local, stats, NEG_FILL), axis=0, keepdims=True)
    factor = jnp.where(split_local & head_lane, jnp.exp(stats - split_top), 0.0)
    split_total = jnp.sum(factor * totals, axis=0, keepdims=True)
    split_part = jnp.sum(dot(factor.astype(BF16), e_ref[...]) * w_ref[...], axis=0, keepdims=True)
    b_send[...] = jnp.zeros_like(b_send)
    b_rows = D // B_COLS
    for i in range(b_rows):
        b_send[i:i + 1, :] = split_part[:, i * B_COLS:(i + 1) * B_COLS]
    b_send[b_rows:b_rows + 1, 0:LANES] = split_top
    b_send[b_rows:b_rows + 1, LANES:2 * LANES] = split_total
    b_targets = [e] + ep_peers
    b_sends = [
        remote(b_send, b_recv.at[e], b_ss.at[k], b_rs.at[e], (mate, peer))
        for k, peer in enumerate(b_targets)
    ]
    for copy in b_sends:
        copy.start()

    for src in ep_peers:
        remote(r_all.at[src], r_all.at[src], r_ss.at[0], r_rs.at[src], (g, src)).wait_recv()
    for s in range(n_ep):
        rows = slice(s * req_dev, (s + 1) * req_dev)
        arrived = r_all[s].astype(F32)
        for i, (low, high) in enumerate(QUARTERS):
            rs_ref[rows, low:high] = arrived[i * req_dev:(i + 1) * req_dev, 0:high - low]
        rt_ref[rows, :] = arrived[ROUTE_PART * req_dev:(ROUTE_PART + 1) * req_dev, ROUTE_COL:PART_COLS]

    expert = e.astype(F32)
    chosen = rt_ref[...]
    has_col = jnp.where((chosen[:, 0:1] == expert) | (chosen[:, 1:2] == expert), 1.0, 0.0)
    r_sub = iota((R, R), 0)
    r_lane = iota((R, R), 1)
    has_row = jnp.sum(jnp.where(r_sub == r_lane, has_col, 0.0), axis=0, keepdims=True)
    earlier = (r_sub < r_lane) & (r_sub // req_dev == r_lane // req_dev)
    rank_row = jnp.sum(jnp.where(earlier, has_col, 0.0), axis=0, keepdims=True)
    slot_sub = iota((slots, R), 0)
    slot_row = iota((slots, R), 1)
    pick = jnp.where(
        (slot_sub // cap == slot_row // req_dev)
        & (has_row > 0.5)
        & (rank_row == (slot_sub % cap).astype(F32)),
        1.0, 0.0,
    ).astype(BF16)

    slot_lane = iota((req_dev, LANES), 1)
    slot_expert = (slot_lane // cap).astype(F32)
    first_hit = slot_expert == routes[0]
    second_hit = slot_expert == routes[1]
    hits = jnp.where(first_hit | second_hit, 1.0, 0.0)
    row_sub = iota((req_dev, LANES), 0)
    rank = jnp.zeros((req_dev, LANES), F32)
    for i in range(req_dev - 1):
        rank = rank + jnp.where(row_sub > i, hits[i:i + 1, :], 0.0)
    blend = jnp.where(first_hit, gates[0], 0.0) + jnp.where(second_hit, gates[1], 0.0)
    blend = jnp.where(rank == (slot_lane % cap).astype(F32), blend, 0.0)

    for src in ep_peers:
        remote(st_all.at[src], st_all.at[src], st_ss.at[0], st_rs.at[src], (g, src)).wait_recv()
    for src in b_targets:
        remote(b_send, b_recv.at[src], b_ss.at[0], b_rs.at[src], (mate, src)).wait_recv()
    extra = NPP - n_pages
    extra_sub = iota((extra, LANES), 0)
    extra_top = jnp.full((extra, LANES), NEG_FILL, F32)
    extra_total = jnp.zeros((extra, LANES), F32)
    for s in range(n_ep):
        extra_top = jnp.where(extra_sub == s, b_recv[s, b_rows:b_rows + 1, 0:LANES], extra_top)
        extra_total = jnp.where(
            extra_sub == s, b_recv[s, b_rows:b_rows + 1, LANES:2 * LANES], extra_total
        )
        for i in range(b_rows):
            row = n_pages + s
            wv_ref[row:row + 1, i * B_COLS:(i + 1) * B_COLS] = b_recv[s, i:i + 1, :]
    all_stats = st_all[...].reshape(n_pages, LANES)
    all_top = jnp.concatenate([all_stats, extra_top], axis=0)
    all_total = jnp.concatenate([pltpu.roll(all_stats, 64, 1), extra_total], axis=0)
    owners = own_ref[...]
    row_top = jnp.zeros((NPP, LANES), F32)
    for r in range(R):
        mine = owners == float(r)
        highest = jnp.max(jnp.where(mine, all_top, NEG_FILL), axis=0, keepdims=True)
        row_top = jnp.where(mine, highest, row_top)
    owned = (owners >= 0.0) & head_lane
    scale = jnp.where(owned, jnp.exp(jnp.where(owned, all_top - row_top, 0.0)), 0.0)
    scaled_total = scale * all_total
    row_total = jnp.ones((NPP, LANES), F32)
    for r in range(R):
        mine = owners == float(r)
        summed = jnp.sum(jnp.where(mine, scaled_total, 0.0), axis=0, keepdims=True)
        row_total = jnp.where(mine, summed, row_total)
    share = jnp.where(owned, scale / jnp.where(owned, row_total, 1.0), 0.0).astype(BF16)

    for c in range(2):
        for src in ep_peers:
            remote(
                a_all.at[c, src], a_all.at[c, src], a_ss.at[c, 0], a_rs.at[c, src], (g, src)
            ).wait_recv()
        for s in range(n_ep):
            arrived = a_all[c, s].astype(F32)
            first = s * PD + c * part_pages
            for i, (low, high) in enumerate(QUARTERS):
                wv_ref[first:first + part_pages, low:high] = (
                    arrived[i * part_pages:(i + 1) * part_pages, 0:high - low]
                )
    attn = []
    for h in range(2):
        columns = slice(h * half, (h + 1) * half)
        terms = (dot(share, e_ref[:, columns]) * wv_ref[:, columns]).astype(BF16)
        attn.append(dot(o_ref[...], terms).astype(BF16))
    stream = [rs_ref[:, h * half:(h + 1) * half] + attn[h].astype(F32) for h in range(2)]
    square = sum(jnp.sum(s * s, axis=1, keepdims=True) for s in stream) * (1.0 / D)
    gain = gain_ref[...].astype(F32).reshape(1, D)
    inverse = lax.rsqrt(square + NORM_EPS)
    normed = [
        (stream[h] * inverse * gain[:, h * half:(h + 1) * half]).astype(BF16)
        for h in range(2)
    ]
    x_all[my_place] = jnp.concatenate([dot(pick, n) for n in normed], axis=0).astype(BF16)

    def x_copy(place, k, device):
        return remote(x_all.at[place], x_all.at[place], x_ss.at[k], x_rs.at[place], device)

    x_sends = [
        x_copy(my_place, k, (2 * peer + side, e)) for k, peer in enumerate(pair_peers)
    ]
    x_sends.append(x_copy(my_place, pairs - 1, (mate, e)))
    for copy in x_sends:
        copy.start()
    own_pick = jnp.where(iota((req_dev, R), 1) == iota((req_dev, R), 0) + e * req_dev, 1.0, 0.0)
    own_attn = [dot(own_pick.astype(BF16), a) for a in attn]
    for k, peer in enumerate(pair_peers):
        x_copy(mine_first + peer, 0, (mate, e)).wait_recv()
        forward = x_copy(mine_first + peer, pairs + k, (mate, e))
        forward.start()
        x_sends.append(forward)
    for copy in w_copies:
        copy.wait()
    for peer in [pair] + pair_peers:
        x_copy(mate_first + peer, 0, (mate, e)).wait_recv()

    rows_in = x_all[...].astype(F32)
    x_lo = rows_in[:, :slots, :].reshape(n_grp * slots, half).astype(BF16)
    x_hi = rows_in[:, slots:, :].reshape(n_grp * slots, half).astype(BF16)
    x_rows = jnp.concatenate([x_lo, x_hi], axis=1)
    gate_part = dot(wg[...], x_rows, ((1,), (1,)))
    up_part = dot(wu[...], x_rows, ((1,), (1,)))
    inner = gate_part / (1.0 + jnp.exp(-gate_part)) * up_part
    inner = jnp.transpose(inner).astype(BF16)

    width = D // CHUNKS
    piece = width // 2
    y_sends = []

    def pair_copy(c):
        return remote(
            y_send.at[c, pl.ds(mate_first, pairs)], y_pair.at[c], p_ss.at[c], p_rs.at[c], (mate, e)
        )

    def pair_sum(c):
        pair_copy(c).wait_recv()
        both = y_send[c, pl.ds(mine_first, pairs)].astype(F32) + y_pair[c].astype(F32)
        y_sum[c] = both.astype(BF16)
        for k, peer in enumerate(pair_peers):
            copy = remote(
                y_sum.at[c, peer], y_recv.at[c, pair], y_ss.at[c, k], y_rs.at[c, pair],
                (2 * peer + side, e),
            )
            copy.start()
            y_sends.append(copy)

    for c in range(CHUNKS):
        y_part = dot(inner, wd[:, c * width:(c + 1) * width])
        for h in range(2):
            y_send[c, :, h * slots:(h + 1) * slots, :] = (
                y_part[:, h * piece:(h + 1) * piece].reshape(n_grp, slots, piece).astype(BF16)
            )
        copy = pair_copy(c)
        copy.start()
        y_sends.append(copy)
        if c:
            pair_sum(c - 1)
    pair_sum(CHUNKS - 1)

    z_sends = []
    for c in range(CHUNKS):
        summed = y_sum[c, pair].astype(F32)
        for src in pair_peers:
            remote(
                y_sum.at[c, src], y_recv.at[c, src], y_ss.at[c, 0], y_rs.at[c, src],
                (2 * src + side, e),
            ).wait_recv()
            summed = summed + y_recv[c, src].astype(F32)
        summed = summed.astype(BF16).astype(F32)
        for s in range(n_ep):
            z_send[c, s, 0:cap, :] = summed[s * cap:(s + 1) * cap, :]
            z_send[c, s, cap:2 * cap, :] = summed[slots + s * cap:slots + (s + 1) * cap, :]
        sends = [
            remote(z_send.at[c, peer], z_recv.at[c, e], z_ss.at[c, k], z_rs.at[c, e], (g, peer))
            for k, peer in enumerate(ep_peers)
        ]
        for copy in sends:
            copy.start()
        z_recv[c, e] = z_send[c, e]
        z_sends += sends
    own_both = jnp.concatenate(own_attn, axis=1)
    for c in range(CHUNKS):
        for src in ep_peers:
            remote(
                z_send.at[c, src], z_recv.at[c, src], z_ss.at[c, 0], z_rs.at[c, src], (g, src)
            ).wait_recv()
        for h in range(2):
            start = c * width + h * piece
            update = own_both[:, start:start + piece]
            for s in range(n_ep):
                for i in range(cap):
                    slot = s * cap + i
                    row = h * cap + i
                    update = update + blend[:, slot:slot + 1] * z_recv[c, s, row:row + 1, :]
            out_ref[:, start:start + piece] = update.astype(BF16)

    for copy in r_sends + exchange + b_sends + x_sends + y_sends + z_sends:
        copy.wait_send()


def on_device(
    n_grp, n_ep,
    queries, residual, gain, key_pages, value_pages, page_table, lengths, split_flag,
    routes, gates, w_gate, w_up, w_down,
):
    req_dev, D = residual.shape
    R = queries.shape[0]
    PD = key_pages.shape[0]
    F = w_gate.shape[2]
    half = D // 2
    cap = max(2, (TOP * req_dev + n_ep - 1) // n_ep)
    slots = n_ep * cap
    n_pages = n_ep * PD
    NPP = -(-(n_pages + n_ep) // 16) * 16
    vmem = pl.BlockSpec(memory_space=pltpu.VMEM)
    smem = pl.BlockSpec(memory_space=pltpu.SMEM)
    hbm = pl.BlockSpec(memory_space=pl.ANY)
    dma = pltpu.SemaphoreType.DMA
    scratch = [
        pltpu.VMEM((PD, PAGE, D), BF16),
        pltpu.VMEM((PD, PAGE, D), BF16),
        pltpu.VMEM((F, D), BF16),
        pltpu.VMEM((F, D), BF16),
        pltpu.VMEM((F, D), BF16),
        pltpu.VMEM((LANES, D), BF16),
        pltpu.VMEM((PD, D), F32),
        pltpu.VMEM((PD, LANES), F32),
        pltpu.VMEM((PD, LANES), F32),
        pltpu.VMEM((PD, D), F32),
        pltpu.VMEM((NPP, LANES), F32),
        pltpu.VMEM((R, NPP), BF16),
        pltpu.VMEM((NPP, D), F32),
        pltpu.VMEM((2 * PD, PART_COLS), F32),
        pltpu.VMEM((R, D), F32),
        pltpu.VMEM((R, LANES), F32),
        pltpu.VMEM((n_ep, 4 * req_dev, PART_COLS), BF16),
        pltpu.VMEM((n_ep, PD, LANES), F32),
        pltpu.VMEM((2, n_ep, 2 * PD, PART_COLS), BF16),
        pltpu.VMEM((8, B_COLS), F32),
        pltpu.VMEM((n_ep, 8, B_COLS), F32),
        pltpu.VMEM((n_grp, 2 * slots, half), BF16),
        pltpu.VMEM((CHUNKS, n_grp, 2 * slots, half // CHUNKS), BF16),
        pltpu.VMEM((CHUNKS, n_grp // 2, 2 * slots, half // CHUNKS), BF16),
        pltpu.VMEM((CHUNKS, n_grp // 2, 2 * slots, half // CHUNKS), BF16),
        pltpu.VMEM((CHUNKS, n_grp // 2, 2 * slots, half // CHUNKS), BF16),
        pltpu.VMEM((CHUNKS, n_ep, 2 * cap, half // CHUNKS), F32),
        pltpu.VMEM((CHUNKS, n_ep, 2 * cap, half // CHUNKS), F32),
        dma((2, PD)),
        dma((3,)),
    ]
    for shape in (
        (n_ep,), (n_ep,), (2, n_ep), (n_ep,), (n_grp,), (CHUNKS,), (CHUNKS, n_grp // 2),
        (CHUNKS, n_ep),
    ):
        scratch += [dma(shape), dma(shape)]
    return pl.pallas_call(
        functools.partial(fused, (n_grp, n_ep, cap)),
        out_shape=jax.ShapeDtypeStruct((req_dev, D), BF16),
        in_specs=[vmem] * 6 + [smem] * 2 + [hbm] * 5,
        out_specs=vmem,
        scratch_shapes=scratch,
        compiler_params=pltpu.CompilerParams(
            collective_id=0, has_side_effects=True, vmem_limit_bytes=56 * 1024 * 1024
        ),
    )(
        queries, residual, gain, page_table, routes.T, gates.T,
        lengths, split_flag,
        key_pages, value_pages, jnp.swapaxes(w_gate, 1, 2), jnp.swapaxes(w_up, 1, 2), w_down,
    )


def solution(mesh):
    in_specs = (
        P("grp", None),
        P(("grp", "ep"), None),
        P(),
        P(("grp", "ep"), None, None),
        P(("grp", "ep"), None, None),
        P("grp", None),
        P("grp"),
        P("grp"),
        P(("grp", "ep"), None),
        P(("grp", "ep"), None),
        P("ep", None, "grp"),
        P("ep", None, "grp"),
        P("ep", "grp", None),
    )
    return jax.shard_map(
        functools.partial(on_device, mesh.shape["grp"], mesh.shape["ep"]),
        mesh=mesh, in_specs=in_specs, out_specs=P(("grp", "ep"), None), check_vma=False,
    )
```

```python
import functools

import jax
import jax.numpy as jnp
from jax import lax
from jax.experimental import pallas as pl
from jax.experimental.pallas import tpu as pltpu
from jax.sharding import PartitionSpec as P

HEAD_DIM = 64
PAGE = 128
LANES = 128
NEG_FILL = -1e30
NEG_FLOOR = -1e29
NORM_EPS = 1e-06
TOP = 2
B_COLS = 256
B_ROWS = 16
STAT_PARTS = 3
CHUNKS = 3
OCTET = 8
V_COLS = 256
QUARTERS = ((0, 640), (640, 1280), (1280, 1792), (1792, 2304))
PART_COLS = 640
ROUTE_PART = 2
ROUTE_COL = 512

F32 = jnp.float32
BF16 = jnp.bfloat16


def iota(shape, axis):
    return lax.broadcasted_iota(jnp.int32, shape, axis)


def dot(a, b, contract=((1,), (0,))):
    return lax.dot_general(a, b, (contract, ((), ())), preferred_element_type=F32)


def fused(
    sizes,
    q_ref, res_ref, gain_ref, pt_ref, routes_ref, gates_ref,
    len_ref, split_ref,
    key_hbm, value_hbm, wg_hbm, wu_hbm, wd_hbm,
    out_ref,
    kbuf, vbuf, wg, wu, wd,
    e_ref, qp_ref, lim_ref, st_ref, w_ref, own_ref, o_ref,
    wv_ref, af_ref, rs_ref, rt_ref,
    r_all, st_all, a_all, b_send, b_recv, x_all, y_send, y_pair, y_sum, y_recv, z_send, z_recv,
    kv_sem, w_sem,
    r_ss, r_rs, st_ss, st_rs, a_ss, a_rs, b_ss, b_rs, x_ss, x_rs, p_ss, p_rs, y_ss, y_rs, z_ss, z_rs,
):
    n_grp, n_ep, cap = sizes
    req_dev, D = res_ref.shape
    R = q_ref.shape[0]
    J = pt_ref.shape[1]
    PD = key_hbm.shape[0]
    half = D // 2
    heads = D // HEAD_DIM
    HP = -(-heads // OCTET) * OCTET
    slots = n_ep * cap
    NPP = own_ref.shape[0]
    n_pages = n_ep * PD

    g = lax.axis_index("grp")
    e = lax.axis_index("ep")
    mate = g + 1 - 2 * lax.rem(g, 2)

    ep_peers = [lax.rem(e + k, n_ep) for k in range(1, n_ep)]
    pairs = n_grp // 2
    side = lax.rem(g, 2)
    pair = lax.div(g, 2)
    pair_peers = [lax.rem(pair + k, pairs) for k in range(1, pairs)]
    mine_first, mate_first = side * pairs, (1 - side) * pairs
    my_place = mine_first + pair

    barrier = pltpu.get_barrier_semaphore()
    for peer in ep_peers:
        pl.semaphore_signal(barrier, inc=1, device_id=(g, peer), device_id_type=pl.DeviceIdType.MESH)
    for peer in pair_peers:
        pl.semaphore_signal(
            barrier, inc=1, device_id=(2 * peer + side, e), device_id_type=pl.DeviceIdType.MESH
        )
    for peer in [e] + ep_peers:
        pl.semaphore_signal(barrier, inc=1, device_id=(mate, peer), device_id_type=pl.DeviceIdType.MESH)

    def kv_copy(p, which):
        source, held = ((key_hbm, kbuf), (value_hbm, vbuf))[which]
        return pltpu.make_async_copy(source.at[p], held.at[p], kv_sem.at[which, p])

    part_pages = PD // 2
    for c in range(2):
        for which in range(2):
            for p in range(c * part_pages, (c + 1) * part_pages):
                kv_copy(p, which).start()
    w_copies = [
        pltpu.make_async_copy(wg_hbm.at[0], wg, w_sem.at[0]),
        pltpu.make_async_copy(wu_hbm.at[0], wu, w_sem.at[1]),
        pltpu.make_async_copy(wd_hbm.at[0], wd, w_sem.at[2]),
    ]

    def remote(src, dst, ss, rs, device):
        return pltpu.make_async_remote_copy(
            src_ref=src, dst_ref=dst, send_sem=ss, recv_sem=rs,
            device_id=device, device_id_type=pl.DeviceIdType.MESH,
        )

    eye = iota((req_dev, req_dev), 0) == iota((req_dev, req_dev), 1)

    def column(row):
        return jnp.sum(jnp.where(eye, row, 0.0), axis=1, keepdims=True)

    routes_t = routes_ref[...].astype(F32)
    gates_t = gates_ref[...].astype(F32)
    routes = [column(routes_t[k:k + 1, :]) for k in range(TOP)]
    gates = [column(gates_t[k:k + 1, :]) for k in range(TOP)]
    route_lane = iota((req_dev, LANES), 1)
    af_ref[...] = jnp.zeros_like(af_ref)
    res = res_ref[...].astype(F32)
    for i, (low, high) in enumerate(QUARTERS):
        af_ref[i * req_dev:(i + 1) * req_dev, 0:high - low] = res[:, low:high]
    af_ref[ROUTE_PART * req_dev:(ROUTE_PART + 1) * req_dev, ROUTE_COL:PART_COLS] = jnp.where(
        route_lane == 0, routes[0], jnp.where(route_lane == 1, routes[1], 0.0)
    )
    r_all[e] = af_ref[...].astype(BF16)

    first_col = iota((LANES, D), 0) * HEAD_DIM
    col = iota((LANES, D), 1)
    in_head = (col >= first_col) & (col < first_col + HEAD_DIM)
    e_ref[...] = jnp.where(in_head, 1.0, 0.0).astype(BF16)
    st_ref[...] = jnp.zeros_like(st_ref)
    wv_ref[n_pages:, :] = jnp.zeros((NPP - n_pages, D), F32)

    split_row = 0
    for r in range(R):
        split_row = split_row + jnp.where(split_ref[r] == 1, r, 0)

    page_id = iota((NPP, J), 0)
    j_start = iota((1, J), 1) * PAGE
    local_id = iota((PD, J), 0) + e * PD
    owner = jnp.full((NPP, J), -1.0, F32)
    own_local = jnp.full((PD, J), -1.0, F32)
    limit = jnp.zeros((PD, J), F32)
    length_col = jnp.zeros((R, 1), jnp.int32)
    split_col = jnp.zeros((R, 1), jnp.int32)
    row_col = iota((R, 1), 0)
    for r in range(R):
        length = len_ref[r]
        entries = jnp.where(j_start < length, pt_ref[r:r + 1, :], -1)
        owner = jnp.where(page_id == entries, float(r), owner)
        hit = local_id == entries
        own_local = jnp.where(hit, float(r), own_local)
        limit = jnp.where(hit, jnp.minimum(length - j_start, PAGE).astype(F32), limit)
        length_col = jnp.where(row_col == r, length, length_col)
        split_col = jnp.where(row_col == r, split_ref[r], split_col)
    owner = jnp.max(owner, axis=1, keepdims=True)
    page_col = iota((NPP, LANES), 0)
    mate_pages = (page_col >= n_pages) & (page_col < n_pages + n_ep)
    own_ref[...] = jnp.where(
        mate_pages, split_row.astype(F32), jnp.broadcast_to(owner, (NPP, LANES))
    )
    own_local = jnp.max(own_local, axis=1, keepdims=True)
    limit = jnp.sum(limit, axis=1, keepdims=True)
    lim_ref[...] = jnp.broadcast_to(limit, (PD, LANES))
    split_local = jnp.broadcast_to(own_local, (PD, LANES)) == split_row.astype(F32)

    page_lane = iota((R, NPP), 1)
    o_rows = jnp.where(
        (page_lane >= n_pages) & (page_lane < n_pages + n_ep) & (split_col == 1), 1.0, 0.0
    )
    for j in range(J):
        entry = jnp.where(length_col > j * PAGE, pt_ref[:, j:j + 1], -1)
        o_rows = jnp.where(page_lane == entry, 1.0, o_rows)
    o_ref[...] = o_rows.astype(BF16)

    queries = q_ref[...].astype(F32)
    page_q = jnp.zeros((PD, D), F32)
    for r in range(R):
        page_q = jnp.where(own_local == float(r), queries[r:r + 1, :], page_q)
    qp_ref[...] = page_q

    token = iota((PAGE, HP), 0).astype(F32)

    def part(c):
        first = c * part_pages
        for p in range(first, first + part_pages):
            kv_copy(p, 0).wait()
        scores = []
        for p in range(first, first + part_pages):
            q_heads = jnp.broadcast_to(qp_ref[p:p + 1, :].astype(BF16), (HP, D)) * e_ref[0:HP, :]
            page_scores = dot(kbuf[p], q_heads, ((1,), (1,))) * HEAD_DIM ** (-0.5)
            scores.append(jnp.where(token < lim_ref[p:p + 1, 0:1], page_scores, NEG_FILL))
        weights = []
        for i in range(part_pages):
            p = first + i
            top = jnp.maximum(jnp.max(scores[i], axis=0, keepdims=True), NEG_FLOOR)
            terms = jnp.exp(scores[i] - top)
            st_ref[p:p + 1, 0:HP] = top
            st_ref[p:p + 1, 64:64 + HP] = jnp.sum(terms, axis=0, keepdims=True)
            weights.append(terms.astype(BF16))
        weights = jnp.concatenate(weights, axis=0)
        for p in range(first, first + part_pages):
            kv_copy(p, 1).wait()
        if c:
            for copy in w_copies:
                copy.start()
        for low in range(0, D, V_COLS):
            columns = slice(low, low + V_COLS)
            spread = dot(weights, e_ref[0:HP, columns]).reshape(part_pages, PAGE, V_COLS)
            w_ref[first:first + part_pages, columns] = jnp.sum(
                spread * vbuf[first:first + part_pages, :, columns].astype(F32), axis=1
            )
        for i, (low, high) in enumerate(QUARTERS):
            af_ref[i * part_pages:(i + 1) * part_pages, 0:high - low] = (
                w_ref[first:first + part_pages, low:high]
            )
        a_all[c, e] = af_ref[...].astype(BF16)

    exchange = []

    def send_part(c):
        for k, peer in enumerate(ep_peers):
            copy = remote(
                a_all.at[c, e], a_all.at[c, e], a_ss.at[c, k], a_rs.at[c, e], (g, peer)
            )
            copy.start()
            exchange.append(copy)

    pl.semaphore_wait(barrier, 2 * n_ep - 1 + pairs - 1)
    r_sends = [
        remote(r_all.at[e], r_all.at[e], r_ss.at[k], r_rs.at[e], (g, peer))
        for k, peer in enumerate(ep_peers)
    ]
    for copy in r_sends:
        copy.start()
    part(0)
    send_part(0)
    part(1)
    send_part(1)

    head_lane = iota((1, LANES), 1) < heads

    stats = st_ref[...]
    st_all[e] = stats
    for k, peer in enumerate(ep_peers):
        copy = remote(st_all.at[e], st_all.at[e], st_ss.at[k], st_rs.at[e], (g, peer))
        copy.start()
        exchange.append(copy)

    totals = pltpu.roll(stats, 64, 1)
    split_top = jnp.max(jnp.where(split_local, stats, NEG_FILL), axis=0, keepdims=True)
    factor = jnp.where(split_local & head_lane, jnp.exp(stats - split_top), 0.0)
    split_total = jnp.sum(factor * totals, axis=0, keepdims=True)
    split_part = jnp.sum(dot(factor.astype(BF16), e_ref[...]) * w_ref[...], axis=0, keepdims=True)
    b_rows = D // B_COLS
    rest = jnp.concatenate([split_top, split_total], axis=1)
    b_parts = [split_part[:, i * B_COLS:(i + 1) * B_COLS] for i in range(b_rows)]
    for _ in range(STAT_PARTS):
        b_parts.append(rest.astype(BF16).astype(F32))
        rest = rest - b_parts[-1]
    b_parts.append(jnp.zeros((B_ROWS - b_rows - STAT_PARTS, B_COLS), F32))
    b_send[...] = jnp.concatenate(b_parts, axis=0).astype(BF16)
    b_targets = [e] + ep_peers
    b_sends = [
        remote(b_send, b_recv.at[e], b_ss.at[k], b_rs.at[e], (mate, peer))
        for k, peer in enumerate(b_targets)
    ]
    for copy in b_sends:
        copy.start()

    for src in ep_peers:
        remote(r_all.at[src], r_all.at[src], r_ss.at[0], r_rs.at[src], (g, src)).wait_recv()
    for s in range(n_ep):
        rows = slice(s * req_dev, (s + 1) * req_dev)
        arrived = r_all[s].astype(F32)
        for i, (low, high) in enumerate(QUARTERS):
            rs_ref[rows, low:high] = arrived[i * req_dev:(i + 1) * req_dev, 0:high - low]
        rt_ref[rows, :] = arrived[ROUTE_PART * req_dev:(ROUTE_PART + 1) * req_dev, ROUTE_COL:PART_COLS]

    expert = e.astype(F32)
    chosen = rt_ref[...]
    has_col = jnp.where((chosen[:, 0:1] == expert) | (chosen[:, 1:2] == expert), 1.0, 0.0)
    r_sub = iota((R, R), 0)
    r_lane = iota((R, R), 1)
    has_row = jnp.sum(jnp.where(r_sub == r_lane, has_col, 0.0), axis=0, keepdims=True)
    earlier = (r_sub < r_lane) & (r_sub // req_dev == r_lane // req_dev)
    rank_row = jnp.sum(jnp.where(earlier, has_col, 0.0), axis=0, keepdims=True)
    slot_sub = iota((slots, R), 0)
    slot_row = iota((slots, R), 1)
    pick = jnp.where(
        (slot_sub // cap == slot_row // req_dev)
        & (has_row > 0.5)
        & (rank_row == (slot_sub % cap).astype(F32)),
        1.0, 0.0,
    ).astype(BF16)

    slot_lane = iota((req_dev, LANES), 1)
    slot_expert = (slot_lane // cap).astype(F32)
    first_hit = slot_expert == routes[0]
    second_hit = slot_expert == routes[1]
    hits = jnp.where(first_hit | second_hit, 1.0, 0.0)
    row_sub = iota((req_dev, LANES), 0)
    rank = jnp.zeros((req_dev, LANES), F32)
    for i in range(req_dev - 1):
        rank = rank + jnp.where(row_sub > i, hits[i:i + 1, :], 0.0)
    blend = jnp.where(first_hit, gates[0], 0.0) + jnp.where(second_hit, gates[1], 0.0)
    blend = jnp.where(rank == (slot_lane % cap).astype(F32), blend, 0.0)

    for src in ep_peers:
        remote(st_all.at[src], st_all.at[src], st_ss.at[0], st_rs.at[src], (g, src)).wait_recv()
    for src in b_targets:
        remote(b_send, b_recv.at[src], b_ss.at[0], b_rs.at[src], (mate, src)).wait_recv()
    extra = NPP - n_pages
    extra_sub = iota((extra, LANES), 0)
    extra_top = jnp.full((extra, LANES), NEG_FILL, F32)
    extra_total = jnp.zeros((extra, LANES), F32)
    for s in range(n_ep):
        arrived = b_recv[s].astype(F32)
        joined = arrived[b_rows:b_rows + 1, :]
        for i in range(1, STAT_PARTS):
            joined = joined + arrived[b_rows + i:b_rows + i + 1, :]
        extra_top = jnp.where(extra_sub == s, joined[:, 0:LANES], extra_top)
        extra_total = jnp.where(extra_sub == s, joined[:, LANES:2 * LANES], extra_total)
        for i in range(b_rows):
            row = n_pages + s
            wv_ref[row:row + 1, i * B_COLS:(i + 1) * B_COLS] = arrived[i:i + 1, :]
    all_stats = st_all[...].reshape(n_pages, LANES)
    all_top = jnp.concatenate([all_stats, extra_top], axis=0)
    all_total = jnp.concatenate([pltpu.roll(all_stats, 64, 1), extra_total], axis=0)
    owners = own_ref[...]
    row_top = jnp.zeros((NPP, LANES), F32)
    for r in range(R):
        mine = owners == float(r)
        highest = jnp.max(jnp.where(mine, all_top, NEG_FILL), axis=0, keepdims=True)
        row_top = jnp.where(mine, highest, row_top)
    owned = (owners >= 0.0) & head_lane
    scale = jnp.where(owned, jnp.exp(jnp.where(owned, all_top - row_top, 0.0)), 0.0)
    scaled_total = scale * all_total
    row_total = jnp.ones((NPP, LANES), F32)
    for r in range(R):
        mine = owners == float(r)
        summed = jnp.sum(jnp.where(mine, scaled_total, 0.0), axis=0, keepdims=True)
        row_total = jnp.where(mine, summed, row_total)
    share = jnp.where(owned, scale / jnp.where(owned, row_total, 1.0), 0.0).astype(BF16)

    for c in range(2):
        for src in ep_peers:
            remote(
                a_all.at[c, src], a_all.at[c, src], a_ss.at[c, 0], a_rs.at[c, src], (g, src)
            ).wait_recv()
        for s in range(n_ep):
            arrived = a_all[c, s].astype(F32)
            first = s * PD + c * part_pages
            for i, (low, high) in enumerate(QUARTERS):
                wv_ref[first:first + part_pages, low:high] = (
                    arrived[i * part_pages:(i + 1) * part_pages, 0:high - low]
                )
    attn = []
    for h in range(2):
        columns = slice(h * half, (h + 1) * half)
        terms = (dot(share, e_ref[:, columns]) * wv_ref[:, columns]).astype(BF16)
        attn.append(dot(o_ref[...], terms).astype(BF16))
    stream = [rs_ref[:, h * half:(h + 1) * half] + attn[h].astype(F32) for h in range(2)]
    square = sum(jnp.sum(s * s, axis=1, keepdims=True) for s in stream) * (1.0 / D)
    gain = gain_ref[...].astype(F32).reshape(1, D)
    inverse = lax.rsqrt(square + NORM_EPS)
    normed = [
        (stream[h] * inverse * gain[:, h * half:(h + 1) * half]).astype(BF16)
        for h in range(2)
    ]
    x_all[my_place] = jnp.concatenate([dot(pick, n) for n in normed], axis=0).astype(BF16)

    def x_copy(place, k, device):
        return remote(x_all.at[place], x_all.at[place], x_ss.at[k], x_rs.at[place], device)

    x_sends = [
        x_copy(my_place, k, (2 * peer + side, e)) for k, peer in enumerate(pair_peers)
    ]
    x_sends.append(x_copy(my_place, pairs - 1, (mate, e)))
    for copy in x_sends:
        copy.start()
    own_pick = jnp.where(iota((req_dev, R), 1) == iota((req_dev, R), 0) + e * req_dev, 1.0, 0.0)
    own_attn = [dot(own_pick.astype(BF16), a) for a in attn]
    for k, peer in enumerate(pair_peers):
        x_copy(mine_first + peer, 0, (mate, e)).wait_recv()
        forward = x_copy(mine_first + peer, pairs + k, (mate, e))
        forward.start()
        x_sends.append(forward)
    for copy in w_copies:
        copy.wait()
    for peer in [pair] + pair_peers:
        x_copy(mate_first + peer, 0, (mate, e)).wait_recv()

    rows_in = x_all[...].astype(F32)
    x_lo = rows_in[:, :slots, :].reshape(n_grp * slots, half).astype(BF16)
    x_hi = rows_in[:, slots:, :].reshape(n_grp * slots, half).astype(BF16)
    x_rows = jnp.concatenate([x_lo, x_hi], axis=1)
    gate_part = dot(wg[...], x_rows, ((1,), (1,)))
    up_part = dot(wu[...], x_rows, ((1,), (1,)))
    inner = gate_part / (1.0 + jnp.exp(-gate_part)) * up_part
    inner = jnp.transpose(inner).astype(BF16)

    width = D // CHUNKS
    piece = width // 2
    y_sends = []

    def pair_copy(c):
        return remote(
            y_send.at[c, pl.ds(mate_first, pairs)], y_pair.at[c], p_ss.at[c], p_rs.at[c], (mate, e)
        )

    def pair_sum(c):
        pair_copy(c).wait_recv()
        both = y_send[c, pl.ds(mine_first, pairs)].astype(F32) + y_pair[c].astype(F32)
        y_sum[c] = both.astype(BF16)
        for k, peer in enumerate(pair_peers):
            copy = remote(
                y_sum.at[c, peer], y_recv.at[c, pair], y_ss.at[c, k], y_rs.at[c, pair],
                (2 * peer + side, e),
            )
            copy.start()
            y_sends.append(copy)

    for c in range(CHUNKS):
        y_part = dot(inner, wd[:, c * width:(c + 1) * width])
        for h in range(2):
            y_send[c, :, h * slots:(h + 1) * slots, :] = (
                y_part[:, h * piece:(h + 1) * piece].reshape(n_grp, slots, piece).astype(BF16)
            )
        copy = pair_copy(c)
        copy.start()
        y_sends.append(copy)
        if c:
            pair_sum(c - 1)
    pair_sum(CHUNKS - 1)

    z_sends = []
    for c in range(CHUNKS):
        summed = y_sum[c, pair].astype(F32)
        for src in pair_peers:
            remote(
                y_sum.at[c, src], y_recv.at[c, src], y_ss.at[c, 0], y_rs.at[c, src],
                (2 * src + side, e),
            ).wait_recv()
            summed = summed + y_recv[c, src].astype(F32)
        summed = summed.astype(BF16).astype(F32)
        for s in range(n_ep):
            z_send[c, s, 0:cap, :] = summed[s * cap:(s + 1) * cap, :]
            z_send[c, s, cap:2 * cap, :] = summed[slots + s * cap:slots + (s + 1) * cap, :]
        sends = [
            remote(z_send.at[c, peer], z_recv.at[c, e], z_ss.at[c, k], z_rs.at[c, e], (g, peer))
            for k, peer in enumerate(ep_peers)
        ]
        for copy in sends:
            copy.start()
        z_recv[c, e] = z_send[c, e]
        z_sends += sends
    own_both = jnp.concatenate(own_attn, axis=1)
    for c in range(CHUNKS):
        for src in ep_peers:
            remote(
                z_send.at[c, src], z_recv.at[c, src], z_ss.at[c, 0], z_rs.at[c, src], (g, src)
            ).wait_recv()
        for h in range(2):
            start = c * width + h * piece
            update = own_both[:, start:start + piece]
            for s in range(n_ep):
                for i in range(cap):
                    slot = s * cap + i
                    row = h * cap + i
                    update = update + blend[:, slot:slot + 1] * z_recv[c, s, row:row + 1, :]
            out_ref[:, start:start + piece] = update.astype(BF16)

    for copy in r_sends + exchange + b_sends + x_sends + y_sends + z_sends:
        copy.wait_send()


def on_device(
    n_grp, n_ep,
    queries, residual, gain, key_pages, value_pages, page_table, lengths, split_flag,
    routes, gates, w_gate, w_up, w_down,
):
    req_dev, D = residual.shape
    R = queries.shape[0]
    PD = key_pages.shape[0]
    F = w_gate.shape[2]
    half = D // 2
    cap = max(2, (TOP * req_dev + n_ep - 1) // n_ep)
    slots = n_ep * cap
    n_pages = n_ep * PD
    NPP = -(-(n_pages + n_ep) // 16) * 16
    vmem = pl.BlockSpec(memory_space=pltpu.VMEM)
    smem = pl.BlockSpec(memory_space=pltpu.SMEM)
    hbm = pl.BlockSpec(memory_space=pl.ANY)
    dma = pltpu.SemaphoreType.DMA
    scratch = [
        pltpu.VMEM((PD, PAGE, D), BF16),
        pltpu.VMEM((PD, PAGE, D), BF16),
        pltpu.VMEM((F, D), BF16),
        pltpu.VMEM((F, D), BF16),
        pltpu.VMEM((F, D), BF16),
        pltpu.VMEM((LANES, D), BF16),
        pltpu.VMEM((PD, D), F32),
        pltpu.VMEM((PD, LANES), F32),
        pltpu.VMEM((PD, LANES), F32),
        pltpu.VMEM((PD, D), F32),
        pltpu.VMEM((NPP, LANES), F32),
        pltpu.VMEM((R, NPP), BF16),
        pltpu.VMEM((NPP, D), F32),
        pltpu.VMEM((2 * PD, PART_COLS), F32),
        pltpu.VMEM((R, D), F32),
        pltpu.VMEM((R, LANES), F32),
        pltpu.VMEM((n_ep, 4 * req_dev, PART_COLS), BF16),
        pltpu.VMEM((n_ep, PD, LANES), F32),
        pltpu.VMEM((2, n_ep, 2 * PD, PART_COLS), BF16),
        pltpu.VMEM((B_ROWS, B_COLS), BF16),
        pltpu.VMEM((n_ep, B_ROWS, B_COLS), BF16),
        pltpu.VMEM((n_grp, 2 * slots, half), BF16),
        pltpu.VMEM((CHUNKS, n_grp, 2 * slots, half // CHUNKS), BF16),
        pltpu.VMEM((CHUNKS, n_grp // 2, 2 * slots, half // CHUNKS), BF16),
        pltpu.VMEM((CHUNKS, n_grp // 2, 2 * slots, half // CHUNKS), BF16),
        pltpu.VMEM((CHUNKS, n_grp // 2, 2 * slots, half // CHUNKS), BF16),
        pltpu.VMEM((CHUNKS, n_ep, 2 * cap, half // CHUNKS), F32),
        pltpu.VMEM((CHUNKS, n_ep, 2 * cap, half // CHUNKS), F32),
        dma((2, PD)),
        dma((3,)),
    ]
    for shape in (
        (n_ep,), (n_ep,), (2, n_ep), (n_ep,), (n_grp,), (CHUNKS,), (CHUNKS, n_grp // 2),
        (CHUNKS, n_ep),
    ):
        scratch += [dma(shape), dma(shape)]
    return pl.pallas_call(
        functools.partial(fused, (n_grp, n_ep, cap)),
        out_shape=jax.ShapeDtypeStruct((req_dev, D), BF16),
        in_specs=[vmem] * 6 + [smem] * 2 + [hbm] * 5,
        out_specs=vmem,
        scratch_shapes=scratch,
        compiler_params=pltpu.CompilerParams(
            collective_id=0, has_side_effects=True, vmem_limit_bytes=56 * 1024 * 1024
        ),
    )(
        queries, residual, gain, page_table, routes.T, gates.T,
        lengths, split_flag,
        key_pages, value_pages, jnp.swapaxes(w_gate, 1, 2), jnp.swapaxes(w_up, 1, 2), w_down,
    )


def solution(mesh):
    in_specs = (
        P("grp", None),
        P(("grp", "ep"), None),
        P(),
        P(("grp", "ep"), None, None),
        P(("grp", "ep"), None, None),
        P("grp", None),
        P("grp"),
        P("grp"),
        P(("grp", "ep"), None),
        P(("grp", "ep"), None),
        P("ep", None, "grp"),
        P("ep", None, "grp"),
        P("ep", "grp", None),
    )
    return jax.shard_map(
        functools.partial(on_device, mesh.shape["grp"], mesh.shape["ep"]),
        mesh=mesh, in_specs=in_specs, out_specs=P(("grp", "ep"), None), check_vma=False,
    )
```
